256 devices in a mesh: dp: 4 (over y), seq: 8 (over z_hi, core), mp: 8 (over x, z_lo).
Axes of the slice: x: 4, y: 4, z: 8 (z_hi: 4, z_lo: 2; z = z_hi * 2 + z_lo), core: 2. Of those that a mesh axis runs over, the one named last changes fastest.
Arguments:
- queries: bfloat16 [32, 4, 32, 8192], P(('dp', 'seq'), None, None, 'mp'), may hold values from -6 to 6
- resp_kv: bfloat16 [32, 4, 32, 2, 1024], P(('dp', 'seq'), None, None, None, 'mp'), may hold values from -8 to 8
- prompt_keys: bfloat16 [4, 1024, 1024], P('dp', 'seq', 'mp'), may hold values from -6 to 6
- prompt_values: bfloat16 [4, 1024, 1024], P('dp', 'seq', 'mp'), may hold values from -6 to 6
- out_weight: bfloat16 [8192, 8192], P('mp', ('dp', 'seq')), may hold values from -3 to 3
- lengths: int32 [32, 4], replicated, may hold values from 8 to 32, as said below
- prompt_of: int32 [32, 4], replicated, may hold values from 0 to 3, each once within a row
Outputs:
- mixed: bfloat16 [4096, 8192], P(('dp', 'seq', 'mp'))
The draws below stay inside these ranges and needn't reach their ends.
Inputs may be any that keep to these rules, and one draw needn't show every extreme that they name: `lengths`: some response has exactly 32 tokens in every draw. `prompt_of`: each source holds exactly one response to every prompt.
All inputs are finite; a program needn't handle non-finite values.
Results may differ from the reference program's by a relative error of at most 0.017.
Values may be sent and summed in bfloat16 or wider, within the bound.
A program may use at most 64 MiB of HBM per device.

```python
import math
import jax
import jax.numpy as jnp
from jax import lax

D = 8192
HEADS = 64
KVH = 8
HD = 128
CAP = 32
PROMPT = 1024
SOURCES = 32
N_DP = 4
N_SEQ = 8
N_MP = 8


def draw_queries(key, part):
    key = jax.random.fold_in(key, 1)
    first = jax.random.fold_in(key, 0)
    shape = (N_DP * N_SEQ, N_DP, CAP, HEADS * HD)
    values = jnp.clip(jax.random.normal(first, shape, jnp.float32), -6.0, 6.0)
    return values.astype(jnp.bfloat16)


def draw_prompt_keys(key, part):
    key = jax.random.fold_in(key, 2)
    first = jax.random.fold_in(key, 0)
    shape = (N_DP, PROMPT, KVH * HD)
    values = jnp.clip(jax.random.normal(first, shape, jnp.float32), -6.0, 6.0)
    return values.astype(jnp.bfloat16)


def draw_lengths(key, part):
    key = jax.random.fold_in(key, 3)
    first, second = jax.random.split(key, 2)
    shape = (N_DP * N_SEQ, N_DP)
    values = jax.random.randint(first, shape, CAP // 4, CAP + 1)
    spot = jax.random.randint(second, (), 0, N_DP * N_SEQ * N_DP)
    flat = values.reshape(-1).at[spot].set(CAP)
    return flat.reshape(shape).astype(jnp.int32)


def levels(stream_key, dims, cuts, least, largest):
    def one(dim, blocks):
        steps = jax.random.uniform(jax.random.fold_in(jax.random.fold_in(stream_key, 6), dim), (blocks,), jnp.float32, least / len(cuts), largest / len(cuts))
        return jnp.repeat(jnp.exp(steps), dims[dim] // blocks).reshape((-1,) + (1,) * (len(dims) - dim - 1))

    factor_of = one(*cuts[0])
    for cut in cuts[1:]:
        factor_of = factor_of * one(*cut)
    return factor_of


def noise(key, extent, deviation, bound, pieces=(), held_as=jnp.bfloat16):
    gain = levels(key, extent, pieces, -0.22, 0.18) if pieces else 1.0
    values = jax.random.normal(key, extent, jnp.float32) * deviation * gain
    return jnp.minimum(jnp.maximum(values, -bound), bound).astype(held_as)


def setup_inputs(seed: int = 0) -> dict:
    splits = jax.random.split(jax.random.key(seed), 8)
    return {
        "queries": draw_queries(jax.random.fold_in(splits[7], 71), 0),
        "resp_kv": noise(splits[1], (SOURCES, N_DP, CAP, 2, KVH * HD), 1.5, 8.0, ((0, 32), (4, 8))),
        "prompt_keys": draw_prompt_keys(jax.random.fold_in(splits[7], 71), 0),
        "prompt_values": noise(splits[3], (N_DP, PROMPT, KVH * HD), 1.0, 6.0, ((0, 4), (1, 8), (2, 8))),
        "out_weight": noise(splits[4], (HEADS * HD, D), (0.9 * (PROMPT / (HEADS * HD)) ** 0.5), 3.0, ((0, 8), (1, 32))),
        "lengths": draw_lengths(jax.random.fold_in(splits[7], 71), 0),
        "prompt_of": jax.vmap(lambda own: jax.random.permutation(own, N_DP))(jax.random.split(splits[6], SOURCES)).reshape((SOURCES, N_DP)).astype(jnp.int32),
    }


def reference(queries, resp_kv, prompt_keys, prompt_values, out_weight, lengths, prompt_of):
    group = HEADS // KVH
    per_group = HEADS // N_MP
    scale = 1.0 / math.sqrt(HD)
    slot_order = jnp.argsort(prompt_of, axis=1).astype(jnp.int32)
    sorted_q = jnp.take_along_axis(queries, slot_order[:, :, None, None], axis=1)
    sorted_kv = jnp.take_along_axis(resp_kv, slot_order[:, :, None, None, None], axis=1)
    sorted_len = jnp.take_along_axis(lengths, slot_order, axis=1)
    arranged_q = sorted_q.reshape(N_DP, N_SEQ, N_DP, CAP, HEADS * HD).transpose(2, 1, 0, 3, 4)
    arranged_q = arranged_q.reshape(N_DP * N_SEQ * N_DP, CAP, HEADS * HD)
    arranged_kv = sorted_kv.reshape(N_DP, N_SEQ, N_DP, CAP, 2, KVH * HD).transpose(2, 1, 0, 3, 4, 5)
    arranged_kv = arranged_kv.reshape(N_DP * N_SEQ * N_DP, CAP, 2, KVH * HD)
    arranged_len = sorted_len.reshape(N_DP, N_SEQ, N_DP).transpose(2, 1, 0).reshape(-1)
    prompt_index = (jnp.arange(N_DP * N_SEQ * N_DP, dtype=jnp.int32) // (N_SEQ * N_DP)).astype(jnp.int32)
    weight_groups = out_weight.reshape(N_MP, per_group * HD, D).astype(jnp.float32)
    positions = jnp.arange(CAP, dtype=jnp.int32)
    causal = positions[:, None] >= positions[None, :]

    def score_one(item):
        query, keyval, length, prompt = item
        cache_k = lax.dynamic_index_in_dim(prompt_keys, prompt, 0, keepdims=False)
        cache_v = lax.dynamic_index_in_dim(prompt_values, prompt, 0, keepdims=False)
        cache_k = cache_k.reshape(PROMPT, KVH, HD).astype(jnp.float32)
        cache_v = cache_v.reshape(PROMPT, KVH, HD).astype(jnp.float32)
        qf = query.reshape(CAP, KVH, group, HD).astype(jnp.float32)
        own_k = keyval[:, 0].reshape(CAP, KVH, HD).astype(jnp.float32)
        own_v = keyval[:, 1].reshape(CAP, KVH, HD).astype(jnp.float32)
        far = jnp.einsum('tkgd,nkd->kgtn', qf, cache_k) * scale
        near = jnp.einsum('tkgd,ukd->kgtu', qf, own_k) * scale
        near = jnp.where(causal, near, -jnp.inf)
        top = jnp.maximum(lax.optimization_barrier(jnp.max(far, axis=-1)), lax.optimization_barrier(jnp.max(near, axis=-1)))
        far_exp = jnp.exp(far - top[..., None])
        near_exp = jnp.exp(near - top[..., None])
        total = lax.optimization_barrier(jnp.sum(far_exp, axis=-1)) + lax.optimization_barrier(jnp.sum(near_exp, axis=-1))
        far_w = lax.optimization_barrier((far_exp / total[..., None]).astype(jnp.bfloat16)).astype(jnp.float32)
        near_w = lax.optimization_barrier((near_exp / total[..., None]).astype(jnp.bfloat16)).astype(jnp.float32)
        attended = jnp.einsum('kgtn,nkd->tkgd', far_w, cache_v) + jnp.einsum('kgtu,ukd->tkgd', near_w, own_v)
        valid = positions < length
        attended = jnp.where(valid[:, None, None, None], attended, 0.0).reshape(CAP, HEADS * HD)
        attended = lax.optimization_barrier(attended.astype(jnp.bfloat16)).astype(jnp.float32)
        parts = jnp.einsum('tmc,mce->mte', attended.reshape(CAP, N_MP, per_group * HD), weight_groups)
        parts = lax.optimization_barrier(parts.astype(jnp.bfloat16)).astype(jnp.float32)
        return lax.optimization_barrier(jnp.sum(parts, axis=0)).astype(jnp.bfloat16)
    mixed = lax.map(score_one, (arranged_q, arranged_kv, arranged_len, prompt_index))
    return mixed.reshape(N_DP * N_SEQ * N_DP * CAP, D)
```

```python
import math

import jax
import jax.numpy as jnp
from jax import lax
from jax.experimental import pallas as pl
from jax.experimental.pallas import tpu as pltpu
from jax.sharding import PartitionSpec as P

HD = 128
MESH = pl.DeviceIdType.MESH
Y_OFF = (0, 1, 3, 2)
X_OFF = (2, 1, 3, 0)


class Ids:
    def __init__(self):
        self.n = 0

    def take(self, *dims):
        base = self.n
        size = math.prod(dims)
        self.n += size

        def at(*idx):
            flat = 0
            for d, i in zip(dims, idx):
                flat = flat * d + i
            return base + flat

        return at


IDS = Ids()
S_Q = IDS.take(4)
S_K = IDS.take(4)
S_V = IDS.take(4)
S_KS = IDS.take(4)
S_VS = IDS.take(4)
S_WSIB = IDS.take(1)
S_WSWAP = IDS.take(2)
S_WRING = IDS.take(2, 2, 2)
S_WSHARE = IDS.take(2, 5)
S_A = IDS.take(4, 4, 2)
S_H = IDS.take(2, 4)
S_F = IDS.take(2, 4)
S_G = IDS.take(2, 8)
N_SEM = IDS.n


def kernel(
    prompt_of, lengths, q_ref, kv_ref, k_ref, v_ref, w_ref, out_ref,
    qs, qb, kb, vb, wb, ab, cs, rh, rf, fs, gb, ss, rs, lsem,
):
    y = lax.axis_index("dp")
    seq = lax.axis_index("seq")
    mp = lax.axis_index("mp")
    zh, c = seq // 2, seq % 2
    x, zl = mp // 2, mp % 2
    z = zh * 2 + zl
    half_k = w_ref.shape[0] // 2
    cap = q_ref.shape[1]
    width = q_ref.shape[2]
    heads = width // HD

    def at_y(off):
        return (lax.rem(y + off, 4), seq, mp)

    def at_x(off):
        return (y, seq, lax.rem(x + off, 4) * 2 + zl)

    def at_z(off):
        zz = lax.rem(z + off, 8)
        return (y, (zz // 2) * 2 + c, x * 2 + zz % 2)

    sibling = (y, zh * 2 + 1 - c, mp)

    def copy(src, dst, send, recv, to):
        return pltpu.make_async_remote_copy(
            src_ref=src, dst_ref=dst, send_sem=ss.at[send], recv_sem=rs.at[recv],
            device_id=to, device_id_type=MESH,
        )

    pending = []

    def send(src, dst, sem, to):
        cp = copy(src, dst, sem, sem, to)
        cp.start()
        pending.append(cp)
        return cp

    def arrived(dst, sem):
        copy(dst, dst, sem, sem, sibling).wait_recv()

    barrier = pltpu.get_barrier_semaphore()
    peers = [at_y(1), at_y(2), at_y(3), sibling, at_x(1), at_x(3)]
    peers += [at_z(m) for m in range(1, 8)]
    peers.append((y, zh * 2 + 1 - c, x * 2 + 1 - zl))
    for peer in peers:
        pl.semaphore_signal(barrier, inc=1, device_id=peer, device_id_type=MESH)

    source = y * 8 + seq
    for k in range(4):
        prompt = lax.rem(y + k, 4)
        slot = jnp.int32(0)
        for j in range(1, 4):
            slot = jnp.where(prompt_of[source, j] == prompt, j, slot)
        if k == 0:
            qb[y, :, 0:width] = q_ref[slot]
            qb[y, :, width : width + 2 * HD] = kv_ref[slot]
        else:
            qs[k, :, 0:width] = q_ref[slot]
            qs[k, :, width : width + 2 * HD] = kv_ref[slot]
    rows_of = lambda s: pl.ds(pl.multiple_of(s * HD, HD), HD)
    kb[rows_of(seq), :] = k_ref[0]
    vb[rows_of(seq), :] = v_ref[0]

    pl.semaphore_wait(barrier, len(peers))

    q_sends = [send(qs.at[k], qb.at[y], S_Q(k), at_y(k)) for k in (2, 1, 3)]
    for m in (2, 1, 3):
        send(kb.at[rows_of(seq)], kb.at[rows_of(seq)], S_K(m), at_z(2 * m))
    for m in (2, 1, 3):
        send(vb.at[rows_of(seq)], vb.at[rows_of(seq)], S_V(m), at_z(2 * m))
    send(kb.at[rows_of(seq)], kb.at[rows_of(seq)], S_KS(0), sibling)
    send(vb.at[rows_of(seq)], vb.at[rows_of(seq)], S_VS(0), sibling)

    keeps = zl == c
    w_local = pltpu.make_async_copy(w_ref, wb.at[y, zl], lsem)
    w_sib = copy(w_ref, wb.at[y, zl], S_WSIB(0), S_WSIB(0), sibling)

    @pl.when(keeps)
    def _():
        w_local.start()
        w_sib.start()
        w_local.wait()

    @pl.when(jnp.logical_not(keeps))
    def _():
        w_sib.wait_recv()

    mine = lambda core: pl.ds(pl.multiple_of(core * half_k, half_k), half_k)
    quarter = half_k // 2
    part = lambda core, h: pl.ds(pl.multiple_of(core * half_k + h * quarter, quarter), quarter)

    def w_start(r, kh):
        block = wb.at[y, kh, mine(c)]
        send(block, block, S_WRING(r, 0, 0), at_y(1))
        send(block, block, S_WRING(r, 0, 1), at_y(3))

    def w_share(r, n, slot):
        send(slot, slot, S_WSHARE(r, n), sibling)

    def w_relay(r, kh):
        left, right = lax.rem(y + 3, 4), lax.rem(y + 1, 4)
        arrived(wb.at[left, kh, mine(c)], S_WRING(r, 0, 0))
        slot = wb.at[left, kh, part(c, 0)]
        send(slot, slot, S_WRING(r, 1, 0), at_y(1))
        w_share(r, 1, wb.at[left, kh, mine(c)])
        arrived(wb.at[right, kh, mine(c)], S_WRING(r, 0, 1))
        slot = wb.at[right, kh, part(c, 1)]
        send(slot, slot, S_WRING(r, 1, 1), at_y(3))
        w_share(r, 2, wb.at[right, kh, mine(c)])

    def w_finish(r, kh):
        far = lax.rem(y + 2, 4)
        for h in range(2):
            slot = wb.at[far, kh, part(c, h)]
            arrived(slot, S_WRING(r, 1, h))
            w_share(r, 3 + h, slot)

    def w_shared(r, n):
        kh = zl if r == 0 else 1 - zl
        other = 1 - c
        if n == 0:
            slot = wb.at[y, kh, mine(other)]
        elif n == 1:
            slot = wb.at[lax.rem(y + 3, 4), kh, mine(other)]
        elif n == 2:
            slot = wb.at[lax.rem(y + 1, 4), kh, mine(other)]
        else:
            slot = wb.at[lax.rem(y + 2, 4), kh, part(other, n - 3)]
        arrived(slot, S_WSHARE(r, n))

    for cp in q_sends:
        cp.wait_send()
        pending.remove(cp)
    w_start(0, zl)

    for m in (1, 3, 2):
        block = rows_of(lax.rem(zh + 4 - m, 4) * 2 + c)
        arrived(kb.at[block], S_K(m))
        send(kb.at[block], kb.at[block], S_KS(m), sibling)
    for m in (1, 3, 2):
        block = rows_of(lax.rem(zh + 4 - m, 4) * 2 + c)
        arrived(vb.at[block], S_V(m))
        send(vb.at[block], vb.at[block], S_VS(m), sibling)

    swaps = []
    for j in range(2):
        rows = pl.ds(j * half_k, half_k)
        swaps.append(
            copy(
                w_ref.at[rows], wb.at[y, zl, rows], S_WSWAP(j), S_WSWAP(0),
                (y, zh * 2 + j, x * 2 + 1 - zl),
            )
        )

    @pl.when(jnp.logical_not(keeps))
    def _():
        for cp in swaps:
            cp.start()

    for m in range(4):
        block = rows_of(lax.rem(zh + 4 - m, 4) * 2 + 1 - c)
        arrived(kb.at[block], S_KS(m))
        arrived(vb.at[block], S_VS(m))

    factor = math.log2(math.e) / math.sqrt(HD)

    def a_slot(i, off, rows=None):
        zz = lax.rem(z + off + 8, 8)
        base = pl.multiple_of((zz // 2) * cap, cap)
        if rows is None:
            return ab.at[i, zz % 2, pl.ds(base, cap)]
        return ab.at[i, zz % 2, pl.ds(pl.multiple_of(base + rows * (cap // 2), cap // 2), cap // 2)]

    def attend(i):
        d = lax.rem(x + X_OFF[i], 4)
        if True:
            for k in (1, 2, 3):
                @pl.when(d == lax.rem(y + 4 - k, 4))
                def _():
                    arrived(qb.at[lax.rem(y + 4 - k, 4)], S_Q(k))
        src = d * 8 + seq
        length = jnp.int32(0)
        for j in range(4):
            length = length + jnp.where(prompt_of[src, j] == y, lengths[src, j], 0)
        q = jnp.concatenate([qb[d, :, h * HD : (h + 1) * HD] for h in range(heads)], axis=0)
        near_k = qb[d, :, width : width + HD]
        near_v = qb[d, :, width + HD : width + 2 * HD]
        nt = (((1,), (1,)), ((), ()))
        far = lax.dot_general(q, kb[...], nt, preferred_element_type=jnp.float32)
        near = lax.dot_general(q, near_k, nt, preferred_element_type=jnp.float32)
        token = lax.rem(lax.broadcasted_iota(jnp.int32, near.shape, 0), cap)
        key = lax.broadcasted_iota(jnp.int32, near.shape, 1)
        near = jnp.where(token >= key, near, -jnp.inf)
        top = jnp.maximum(
            jnp.max(far, axis=1, keepdims=True), jnp.max(near, axis=1, keepdims=True)
        )
        far = jnp.exp2((far - top) * factor)
        near = jnp.exp2((near - top) * factor)
        total = jnp.sum(far, axis=1, keepdims=True) + jnp.sum(near, axis=1, keepdims=True)
        result = jnp.dot(far.astype(jnp.bfloat16), vb[...], preferred_element_type=jnp.float32)
        result = result + jnp.dot(
            near.astype(jnp.bfloat16), near_v, preferred_element_type=jnp.float32
        )
        row = lax.rem(lax.broadcasted_iota(jnp.int32, result.shape, 0), cap)
        result = jnp.where(row < length, result / total, 0.0).astype(jnp.bfloat16)
        base = pl.multiple_of(zh * cap, cap)
        for h in range(heads):
            ab[i, zl, pl.ds(base, cap), h * HD : (h + 1) * HD] = result[h * cap : (h + 1) * cap]
        slot = a_slot(i, 0)
        send(slot, slot, S_A(i, 0, 0), at_z(1))
        send(slot, slot, S_A(i, 0, 1), at_z(7))

    def a_relay(i, s):
        slot = a_slot(i, -s)
        arrived(slot, S_A(i, s - 1, 0))
        if s == 3:
            slot = a_slot(i, -s, 0)
        send(slot, slot, S_A(i, s, 0), at_z(1))
        slot = a_slot(i, s)
        arrived(slot, S_A(i, s - 1, 1))
        if s == 3:
            slot = a_slot(i, s, 1)
        send(slot, slot, S_A(i, s, 1), at_z(7))

    def product(i, k):
        yk = lax.rem(y + Y_OFF[k], 4)
        return jnp.dot(ab[i, 0], wb[yk, 0], preferred_element_type=jnp.float32) + jnp.dot(
            ab[i, 1], wb[yk, 1], preferred_element_type=jnp.float32
        )

    def w_needed(k):
        if k == 0:
            w_shared(1, 0)
        elif k == 1:
            w_shared(0, 2)
            w_shared(1, 2)
        elif k == 2:
            w_shared(0, 1)
            w_shared(1, 1)
        else:
            w_finish(1, 1 - zl)
            for r in range(2):
                w_shared(r, 3)
                w_shared(r, 4)

    rows = cs.shape[2]
    half = rows // 2

    def project(i):
        a_far = [a_slot(i, 4, h) for h in range(2)]
        arrived(a_far[0], S_A(i, 3, 0))
        arrived(a_far[1], S_A(i, 3, 1))
        for k in range(4):
            if i == 0:
                w_needed(k)
            value = product(i, k)
            if i == 0:
                cs[0, k] = value.astype(jnp.bfloat16)
                send(cs.at[0, k, 0:half], rh.at[0, k], S_H(0, k), at_x(1))
                send(cs.at[0, k, half:rows], rh.at[1, k], S_H(1, k), at_x(3))
            elif i == 1:
                arrived(rh.at[0, k], S_H(0, k))
                top = value[0:half] + rh[0, k].astype(jnp.float32)
                cs[1, k, 0:half] = top.astype(jnp.bfloat16)
                cs[1, k, half:rows] = value[half:rows].astype(jnp.bfloat16)
                send(cs.at[1, k], rf.at[0, k], S_F(0, k), at_x(1))
            elif i == 2:
                arrived(rh.at[1, k], S_H(1, k))
                low = value[half:rows] + rh[1, k].astype(jnp.float32)
                cs[2, k, 0:half] = value[0:half].astype(jnp.bfloat16)
                cs[2, k, half:rows] = low.astype(jnp.bfloat16)
                send(cs.at[2, k], rf.at[1, k], S_F(1, k), at_x(3))
            else:
                arrived(rf.at[0, k], S_F(0, k))
                arrived(rf.at[1, k], S_F(1, k))
                value = value + rf[0, k].astype(jnp.float32) + rf[1, k].astype(jnp.float32)
                fs[k] = value.astype(jnp.bfloat16)
                if k % 2 == 1:
                    g = k // 2
                    for m in range(1, 8):
                        zz = lax.rem(z + m, 8)
                        block = pl.ds(pl.multiple_of(zz * 16, 16), 16)
                        send(
                            fs.at[2 * g : 2 * g + 2, block], gb.at[2 * g : 2 * g + 2, z],
                            S_G(g, m), at_z(m),
                        )

    for t in range(8):
        if t < 4:
            attend(t)
        for s in (3, 2, 1):
            if 0 <= t - s < 4:
                a_relay(t - s, s)
        if t == 1:
            arrived(wb.at[y, 1 - zl, mine(c)], S_WSWAP(0))
            w_start(1, 1 - zl)
            w_share(1, 0, wb.at[y, 1 - zl, mine(c)])
            w_relay(0, zl)
        if t == 3:
            w_finish(0, zl)
            w_relay(1, 1 - zl)
        if t >= 4:
            project(t - 4)

    for g in range(2):
        for k in (2 * g, 2 * g + 1):
            yk = lax.rem(y + Y_OFF[k], 4)
            own = pl.ds(pl.multiple_of(z * 16, 16), 16)
            gb[k, z] = fs[k, own]
        for m in range(1, 8):
            zz = lax.rem(z + 8 - m, 8)
            arrived(gb.at[2 * g : 2 * g + 2, zz], S_G(g, m))
        for k in (2 * g, 2 * g + 1):
            yk = lax.rem(y + Y_OFF[k], 4)
            for zz in range(8):
                columns = pl.ds(pl.multiple_of((yk * 8 + zz) * 256, 256), 256)
                out_ref[:, columns] = gb[k, zz]

    for cp in pending:
        cp.wait_send()

    @pl.when(keeps)
    def _():
        w_sib.wait_send()

    @pl.when(jnp.logical_not(keeps))
    def _():
        for cp in swaps:
            cp.wait_send()


def local(queries, resp_kv, prompt_keys, prompt_values, out_weight, lengths, prompt_of):
    slots, cap, width = queries.shape[1:]
    tokens = prompt_keys.shape[1]
    k_rows, columns = out_weight.shape
    q = queries.reshape(slots, cap, width)
    kv = resp_kv.reshape(slots, cap, 2 * HD)
    packed = width + 2 * HD
    bf = jnp.bfloat16
    vmem = pl.BlockSpec(memory_space=pltpu.VMEM)
    smem = pl.BlockSpec(memory_space=pltpu.SMEM)
    return pl.pallas_call(
        kernel,
        out_shape=jax.ShapeDtypeStruct((16, 32 * columns), bf),
        in_specs=[smem, smem, vmem, vmem, vmem, vmem, pl.BlockSpec(memory_space=pl.ANY)],
        out_specs=vmem,
        scratch_shapes=[
            pltpu.VMEM((4, cap, packed), bf),
            pltpu.VMEM((4, cap, packed), bf),
            pltpu.VMEM((8 * tokens, HD), bf),
            pltpu.VMEM((8 * tokens, HD), bf),
            pltpu.VMEM((4, 2, k_rows, columns), bf),
            pltpu.VMEM((4, 2, 4 * cap, width), bf),
            pltpu.VMEM((3, 4, 4 * cap, columns), bf),
            pltpu.VMEM((2, 4, 2 * cap, columns), bf),
            pltpu.VMEM((2, 4, 4 * cap, columns), bf),
            pltpu.VMEM((4, 4 * cap, columns), bf),
            pltpu.VMEM((4, 8, 16, columns), bf),
            pltpu.SemaphoreType.DMA((N_SEM,)),
            pltpu.SemaphoreType.DMA((N_SEM,)),
            pltpu.SemaphoreType.DMA,
        ],
        compiler_params=pltpu.CompilerParams(
            collective_id=0, has_side_effects=True, vmem_limit_bytes=48 * 2**20
        ),
        cost_estimate=pl.CostEstimate(
            flops=2_700_000_000, bytes_accessed=2_000_000, transcendentals=1_100_000
        ),
        name="attend_project",
    )(prompt_of, lengths, q, kv, prompt_keys, prompt_values, out_weight)


def solution(mesh):
    placed = (
        P(("dp", "seq"), None, None, "mp"),
        P(("dp", "seq"), None, None, None, "mp"),
        P("dp", "seq", "mp"),
        P("dp", "seq", "mp"),
        P("mp", ("dp", "seq")),
        P(),
        P(),
    )
    return jax.shard_map(
        local, mesh=mesh, in_specs=placed, out_specs=P(("dp", "seq", "mp"), None), check_vma=False
    )
```

```python
import math

import jax
import jax.numpy as jnp
from jax import lax
from jax.experimental import pallas as pl
from jax.experimental.pallas import tpu as pltpu
from jax.sharding import PartitionSpec as P

HD = 128
MESH = pl.DeviceIdType.MESH
Y_OFF = (0, 1, 3, 2)
BATCHES = ((0, 1), (2, 3))
GROUPS = ((0, 3), (3, 4))


class Ids:
    def __init__(self):
        self.n = 0

    def take(self, *dims):
        base = self.n
        size = math.prod(dims)
        self.n += size

        def at(*idx):
            flat = 0
            for d, i in zip(dims, idx):
                flat = flat * d + i
            return base + flat

        return at


IDS = Ids()
S_Q = IDS.take(4)
S_K = IDS.take(4)
S_V = IDS.take(4)
S_KS = IDS.take(4)
S_VS = IDS.take(4)
S_WSIB = IDS.take(1)
S_WSWAP = IDS.take(2)
S_WRING = IDS.take(2, 2, 2)
S_WSHARE = IDS.take(2, 5)
S_A = IDS.take(len(BATCHES), 4, 2)
S_R = IDS.take(4, len(GROUPS), 4)
S_G = IDS.take(len(GROUPS), 8)
N_SEM = IDS.n


def kernel(
    prompt_hbm, length_hbm, q_hbm, kv_hbm, k_hbm, v_hbm, w_ref, out_ref,
    prompt_of, lengths, q_ref, kv_ref,
    qs, qb, kb, vb, wb, ab, cs, rb, fs, gb, ss, rs, lsem,
):
    y = lax.axis_index("dp")
    seq = lax.axis_index("seq")
    mp = lax.axis_index("mp")
    zh, c = seq // 2, seq % 2
    x, zl = mp // 2, mp % 2
    z = zh * 2 + zl
    half_k = w_ref.shape[0] // 2
    columns = w_ref.shape[1]
    cap = q_ref.shape[1]
    width = q_ref.shape[2]
    heads = width // HD
    half_cap = cap // 2

    def at_y(off):
        return (lax.rem(y + off, 4), seq, mp)

    def at_x(off):
        return (y, seq, lax.rem(x + off, 4) * 2 + zl)

    def at_z(off):
        zz = lax.rem(z + off, 8)
        return (y, (zz // 2) * 2 + c, x * 2 + zz % 2)

    sibling = (y, zh * 2 + 1 - c, mp)

    def copy(src, dst, send, recv, to):
        return pltpu.make_async_remote_copy(
            src_ref=src, dst_ref=dst, send_sem=ss.at[send], recv_sem=rs.at[recv],
            device_id=to, device_id_type=MESH,
        )

    pending = []

    def send(src, dst, sem, to):
        cp = copy(src, dst, sem, sem, to)
        cp.start()
        pending.append(cp)
        return cp

    def arrived(dst, sem):
        copy(dst, dst, sem, sem, sibling).wait_recv()

    rows_of = lambda s: pl.ds(pl.multiple_of(s * HD, HD), HD)
    own_rows = rows_of(seq)
    fetches = [
        pltpu.make_async_copy(src, dst, lsem.at[n])
        for n, (src, dst) in enumerate(
            (
                (prompt_hbm, prompt_of),
                (length_hbm, lengths),
                (q_hbm.at[0], q_ref),
                (kv_hbm.at[0], kv_ref),
                (k_hbm.at[0], kb.at[own_rows]),
                (v_hbm.at[0], vb.at[own_rows]),
            )
        )
    ]
    for cp in fetches:
        cp.start()
    keeps = zl == c
    w_local = pltpu.make_async_copy(w_ref, wb.at[y, zl], lsem.at[len(fetches)])

    @pl.when(keeps)
    def _():
        w_local.start()

    barrier = pltpu.get_barrier_semaphore()
    peers = [at_y(1), at_y(2), at_y(3), sibling, at_x(1), at_x(2), at_x(3)]
    peers += [at_z(m) for m in range(1, 8)]
    peers.append((y, zh * 2 + 1 - c, x * 2 + 1 - zl))
    for peer in peers:
        pl.semaphore_signal(barrier, inc=1, device_id=peer, device_id_type=MESH)

    for cp in fetches:
        cp.wait()
    source = y * 8 + seq
    for k in range(4):
        prompt = lax.rem(y + k, 4)
        slot = jnp.int32(0)
        for j in range(1, 4):
            slot = jnp.where(prompt_of[j, source] == prompt, j, slot)
        to, at = (qb, y) if k == 0 else (qs, k)
        to[at, :, 0:width] = q_ref[slot]
        pair = kv_ref[slot]
        to[at, :, width : width + HD] = pair[:, 0, :]
        to[at, :, width + HD : width + 2 * HD] = pair[:, 1, :]

    pl.semaphore_wait(barrier, len(peers))

    for m in (2, 1, 3):
        send(kb.at[own_rows], kb.at[own_rows], S_K(m), at_z(2 * m))
    for k in (2, 1, 3):
        send(qs.at[k], qb.at[y], S_Q(k), at_y(k))
    for m in (2, 1, 3):
        send(vb.at[own_rows], vb.at[own_rows], S_V(m), at_z(2 * m))
    send(kb.at[own_rows], kb.at[own_rows], S_KS(0), sibling)
    send(vb.at[own_rows], vb.at[own_rows], S_VS(0), sibling)

    w_sib = copy(w_ref, wb.at[y, zl], S_WSIB(0), S_WSIB(0), sibling)

    @pl.when(keeps)
    def _():
        w_sib.start()
        w_local.wait()

    @pl.when(jnp.logical_not(keeps))
    def _():
        w_sib.wait_recv()

    mine = lambda core: pl.ds(pl.multiple_of(core * half_k, half_k), half_k)
    quarter = half_k // 2
    part = lambda core, h: pl.ds(pl.multiple_of(core * half_k + h * quarter, quarter), quarter)
    late = 1 - zl

    def w_start(r, kh):
        block = wb.at[y, kh, mine(c)]
        send(block, block, S_WRING(r, 0, 0), at_y(1))
        send(block, block, S_WRING(r, 0, 1), at_y(3))

    def w_share(r, n, slot):
        send(slot, slot, S_WSHARE(r, n), sibling)

    def w_relay(r, kh):
        left, right = lax.rem(y + 3, 4), lax.rem(y + 1, 4)
        arrived(wb.at[left, kh, mine(c)], S_WRING(r, 0, 0))
        slot = wb.at[left, kh, part(c, 0)]
        send(slot, slot, S_WRING(r, 1, 0), at_y(1))
        w_share(r, 1, wb.at[left, kh, mine(c)])
        arrived(wb.at[right, kh, mine(c)], S_WRING(r, 0, 1))
        slot = wb.at[right, kh, part(c, 1)]
        send(slot, slot, S_WRING(r, 1, 1), at_y(3))
        w_share(r, 2, wb.at[right, kh, mine(c)])

    def w_finish(r, kh):
        far = lax.rem(y + 2, 4)
        for h in range(2):
            slot = wb.at[far, kh, part(c, h)]
            arrived(slot, S_WRING(r, 1, h))
            w_share(r, 3 + h, slot)

    def w_shared(r, n):
        kh = zl if r == 0 else 1 - zl
        other = 1 - c
        if n == 0:
            slot = wb.at[y, kh, mine(other)]
        elif n == 1:
            slot = wb.at[lax.rem(y + 3, 4), kh, mine(other)]
        elif n == 2:
            slot = wb.at[lax.rem(y + 1, 4), kh, mine(other)]
        else:
            slot = wb.at[lax.rem(y + 2, 4), kh, part(other, n - 3)]
        arrived(slot, S_WSHARE(r, n))

    def w_near():
        w_shared(1, 0)
        for r in range(2):
            w_shared(r, 1)
            w_shared(r, 2)

    def w_far():
        for r in range(2):
            w_shared(r, 3)
            w_shared(r, 4)

    def forward(ref, first, then):
        for m in (1, 3, 2):
            block = rows_of(lax.rem(zh + 4 - m, 4) * 2 + c)
            arrived(ref.at[block], first(m))
            send(ref.at[block], ref.at[block], then(m), sibling)

    def shared(ref, then):
        for m in range(4):
            block = rows_of(lax.rem(zh + 4 - m, 4) * 2 + 1 - c)
            arrived(ref.at[block], then(m))

    swaps = []
    for j in range(2):
        rows = pl.ds(j * half_k, half_k)
        swaps.append(
            copy(
                w_ref.at[rows], wb.at[y, zl, rows], S_WSWAP(j), S_WSWAP(0),
                (y, zh * 2 + j, x * 2 + 1 - zl),
            )
        )

    def swap_start():
        @pl.when(jnp.logical_not(keeps))
        def _():
            for cp in swaps:
                cp.start()

    def swap_end():
        arrived(wb.at[y, late, mine(c)], S_WSWAP(0))
        w_start(1, late)
        w_share(1, 0, wb.at[y, late, mine(c)])

    factor = math.log2(math.e) / math.sqrt(HD)

    def attend(i):
        d = lax.rem(y + Y_OFF[i], 4)
        if i:
            arrived(qb.at[d], S_Q((4 - Y_OFF[i]) % 4))
        src = d * 8 + seq
        length = jnp.int32(0)
        for j in range(4):
            length = length + jnp.where(prompt_of[j, src] == y, lengths[j, src], 0)
        q = jnp.concatenate([qb[d, :, h * HD : (h + 1) * HD] for h in range(heads)], axis=0)
        near_k = qb[d, :, width : width + HD]
        near_v = qb[d, :, width + HD : width + 2 * HD]
        nt = (((1,), (1,)), ((), ()))
        far = lax.dot_general(q, kb[...], nt, preferred_element_type=jnp.float32)
        near = lax.dot_general(q, near_k, nt, preferred_element_type=jnp.float32)
        token = lax.rem(lax.broadcasted_iota(jnp.int32, near.shape, 0), cap)
        key = lax.broadcasted_iota(jnp.int32, near.shape, 1)
        near = jnp.where(token >= key, near, -jnp.inf)
        top = jnp.maximum(
            jnp.max(far, axis=1, keepdims=True), jnp.max(near, axis=1, keepdims=True)
        )
        far = jnp.exp2((far - top) * factor)
        near = jnp.exp2((near - top) * factor)
        total = jnp.sum(far, axis=1, keepdims=True) + jnp.sum(near, axis=1, keepdims=True)
        result = jnp.dot(far.astype(jnp.bfloat16), vb[...], preferred_element_type=jnp.float32)
        result = result + jnp.dot(
            near.astype(jnp.bfloat16), near_v, preferred_element_type=jnp.float32
        )
        row = lax.rem(lax.broadcasted_iota(jnp.int32, result.shape, 0), cap)
        result = jnp.where(row < length, result / total, 0.0).astype(jnp.bfloat16)
        for h in range(heads):
            ab[zh, zl, i * cap : (i + 1) * cap, h * HD : (h + 1) * HD] = (
                result[h * cap : (h + 1) * cap]
            )

    def a_slot(b, off, h=None):
        zz = lax.rem(z + off + 8, 8)
        first, size = BATCHES[b][0] * cap, len(BATCHES[b]) * cap
        if h is not None:
            size = size // 2
            first = first + h * size
        return ab.at[zz // 2, zz % 2, first : first + size]

    def a_start(b):
        for i in BATCHES[b]:
            attend(i)
        slot = a_slot(b, 0)
        send(slot, slot, S_A(b, 0, 0), at_z(1))
        send(slot, slot, S_A(b, 0, 1), at_z(7))

    def a_relay(b, s):
        slot = a_slot(b, -s)
        arrived(slot, S_A(b, s - 1, 0))
        if s == 3:
            slot = a_slot(b, -s, 0)
        send(slot, slot, S_A(b, s, 0), at_z(1))
        slot = a_slot(b, s)
        arrived(slot, S_A(b, s - 1, 1))
        if s == 3:
            slot = a_slot(b, s, 1)
        send(slot, slot, S_A(b, s, 1), at_z(7))

    def a_last(b):
        for h in range(2):
            arrived(a_slot(b, 4, h), S_A(b, 3, h))

    def pair(p):
        off = (0, 3 - 2 * zl, 1 + 2 * zl, 2)[p]
        return lax.rem(zh + off, 4)

    def cols(g):
        first, last = GROUPS[g]
        return slice(first * columns, last * columns)

    def chunk_of(xx):
        u = lax.rem(xx - y + 4, 4)
        return u + u // 2 - 2 * (u // 2) * (u % 2)

    def block_of(xx):
        return pl.ds(pl.multiple_of(chunk_of(xx) * cap, cap), cap)

    def project(p, g):
        zz = pair(p)
        for k in range(*GROUPS[g]):
            yk = lax.rem(y + Y_OFF[k], 4)
            value = jnp.dot(ab[zz, 0], wb[yk, 0], preferred_element_type=jnp.float32)
            value = value + jnp.dot(ab[zz, 1], wb[yk, 1], preferred_element_type=jnp.float32)
            cs[p, :, k * columns : (k + 1) * columns] = value.astype(jnp.bfloat16)
        for off in (2, 1, 3):
            rows = block_of(lax.rem(x + off, 4))
            send(
                cs.at[p, rows, cols(g)], rb.at[p, off, :, cols(g)], S_R(p, g, off), at_x(off)
            )

    def reduce(p, g):
        value = cs[p, block_of(x), cols(g)].astype(jnp.float32)
        for off in (1, 3, 2):
            arrived(rb.at[p, off, :, cols(g)], S_R(p, g, off))
            value = value + rb[p, off, :, cols(g)].astype(jnp.float32)
        fs[p, :, cols(g)] = value.astype(jnp.bfloat16)
        zz = pair(p)
        for t in range(2):
            half = slice(t * half_cap, (t + 1) * half_cap)
            if p == 0:
                @pl.when(zl == t)
                def _():
                    gb[z, :, cols(g)] = fs[p, half, cols(g)]
        if p == 0:
            half = pl.ds(pl.multiple_of(late * half_cap, half_cap), half_cap)
            off = 1 + 6 * zl
            send(
                fs.at[p, half, cols(g)], gb.at[z, :, cols(g)], S_G(g, 0) + off,
                (y, zz * 2 + c, x * 2 + late),
            )
        else:
            for t in range(2):
                half = slice(t * half_cap, (t + 1) * half_cap)
                off = lax.rem(zz * 2 + t - z + 8, 8)
                send(
                    fs.at[p, half, cols(g)], gb.at[z, :, cols(g)], S_G(g, 0) + off,
                    (y, zz * 2 + c, x * 2 + t),
                )

    def collect(g):
        for m in range(8):
            zz = lax.rem(z + 8 - m, 8)
            if m:
                arrived(gb.at[zz, :, cols(g)], S_G(g, 0) + m)
        for k in range(*GROUPS[g]):
            yk = lax.rem(y + Y_OFF[k], 4)
            for zz in range(8):
                place = pl.ds(pl.multiple_of((yk * 8 + zz) * columns, columns), columns)
                out_ref[:, place] = gb[zz, :, k * columns : (k + 1) * columns]

    batches = range(len(BATCHES))
    w_start(0, zl)
    swap_start()
    forward(kb, S_K, S_KS)
    forward(vb, S_V, S_VS)
    shared(kb, S_KS)
    shared(vb, S_VS)
    for b in batches:
        a_start(b)
    swap_end()
    for b in batches:
        a_relay(b, 1)
    w_relay(0, zl)
    for b in batches:
        a_relay(b, 2)
    w_relay(1, late)
    w_near()
    project(0, 0)
    project(1, 0)
    for b in batches:
        a_relay(b, 3)
    reduce(0, 0)
    reduce(1, 0)
    project(2, 0)
    w_finish(0, zl)
    w_finish(1, late)
    w_far()
    project(0, 1)
    project(1, 1)
    project(2, 1)
    reduce(2, 0)
    for b in batches:
        a_last(b)
    project(3, 0)
    project(3, 1)
    reduce(0, 1)
    reduce(1, 1)
    reduce(2, 1)
    reduce(3, 0)
    reduce(3, 1)
    collect(0)
    collect(1)

    for cp in pending:
        cp.wait_send()

    @pl.when(keeps)
    def _():
        w_sib.wait_send()

    @pl.when(jnp.logical_not(keeps))
    def _():
        for cp in swaps:
            cp.wait_send()


def local(queries, resp_kv, prompt_keys, prompt_values, out_weight, lengths, prompt_of):
    slots, cap, width = queries.shape[1:]
    tokens = prompt_keys.shape[1]
    k_rows, columns = out_weight.shape
    packed = width + 2 * HD
    bf = jnp.bfloat16
    hbm = pl.BlockSpec(memory_space=pltpu.HBM)
    return pl.pallas_call(
        kernel,
        out_shape=jax.ShapeDtypeStruct((16, 32 * columns), bf),
        in_specs=[hbm] * 7,
        out_specs=pl.BlockSpec(memory_space=pltpu.VMEM),
        scratch_shapes=[
            pltpu.SMEM(prompt_of.shape[::-1], jnp.int32),
            pltpu.SMEM(lengths.shape[::-1], jnp.int32),
            pltpu.VMEM((slots, cap, width), bf),
            pltpu.VMEM((slots, cap, 2, HD), bf),
            pltpu.VMEM((4, cap, packed), bf),
            pltpu.VMEM((4, cap, packed), bf),
            pltpu.VMEM((8 * tokens, HD), bf),
            pltpu.VMEM((8 * tokens, HD), bf),
            pltpu.VMEM((4, 2, k_rows, columns), bf),
            pltpu.VMEM((4, 2, 4 * cap, width), bf),
            pltpu.VMEM((4, 4 * cap, 4 * columns), bf),
            pltpu.VMEM((4, 4, cap, 4 * columns), bf),
            pltpu.VMEM((4, cap, 4 * columns), bf),
            pltpu.VMEM((8, cap // 2, 4 * columns), bf),
            pltpu.SemaphoreType.DMA((N_SEM,)),
            pltpu.SemaphoreType.DMA((N_SEM,)),
            pltpu.SemaphoreType.DMA((8,)),
        ],
        compiler_params=pltpu.CompilerParams(
            collective_id=0, has_side_effects=True, vmem_limit_bytes=48 * 2**20
        ),
        cost_estimate=pl.CostEstimate(
            flops=2_700_000_000, bytes_accessed=2_000_000, transcendentals=1_100_000
        ),
        name="attend_project",
    )(*[
        pltpu.with_memory_space_constraint(a, pltpu.HBM)
        for a in (
            prompt_of.T, lengths.T, queries, resp_kv, prompt_keys, prompt_values, out_weight
        )
    ])


def solution(mesh):
    placed = (
        P(("dp", "seq"), None, None, "mp"),
        P(("dp", "seq"), None, None, None, "mp"),
        P("dp", "seq", "mp"),
        P("dp", "seq", "mp"),
        P("mp", ("dp", "seq")),
        P(),
        P(),
    )
    return jax.shard_map(
        local, mesh=mesh, in_specs=placed, out_specs=P(("dp", "seq", "mp"), None), check_vma=False
    )
```

```python
import math

import jax
import jax.numpy as jnp
from jax import lax
from jax.experimental import pallas as pl
from jax.experimental.pallas import tpu as pltpu
from jax.sharding import PartitionSpec as P

HD = 128
MESH = pl.DeviceIdType.MESH
Y_OFF = (0, 1, 3, 2)
BATCHES = ((0, 1), (2, 3))
GROUPS = ((0, 3), (3, 4))
LAST = ((0, 1), (1, 2), (2, 3), (3, 4))


class Ids:
    def __init__(self):
        self.n = 0

    def take(self, *dims):
        base = self.n
        size = math.prod(dims)
        self.n += size

        def at(*idx):
            flat = 0
            for d, i in zip(dims, idx):
                flat = flat * d + i
            return base + flat

        return at


IDS = Ids()
S_Q = IDS.take(4)
S_K = IDS.take(4)
S_KS = IDS.take(4)
S_WSIB = IDS.take(1)
S_WSWAP = IDS.take(2)
S_WRING = IDS.take(2, 2, 2)
S_WSHARE = IDS.take(2, 5)
S_A = IDS.take(len(BATCHES), 4, 2)
S_R = IDS.take(4, 4, 4)
S_G = IDS.take(4, 8)
N_SEM = IDS.n


def kernel(
    prompt_hbm, length_hbm, q_hbm, kv_hbm, k_hbm, v_hbm, w_ref, out_ref,
    prompt_of, lengths, q_ref, kv_ref,
    qs, qb, kb, wb, ab, cs, rb, fs, gb, ss, rs, lsem,
):
    y = lax.axis_index("dp")
    seq = lax.axis_index("seq")
    mp = lax.axis_index("mp")
    zh, c = seq // 2, seq % 2
    x, zl = mp // 2, mp % 2
    z = zh * 2 + zl
    half_k = w_ref.shape[0] // 2
    columns = w_ref.shape[1]
    cap = q_ref.shape[1]
    width = q_ref.shape[2]
    heads = width // HD
    half_cap = cap // 2

    def at_y(off):
        return (lax.rem(y + off, 4), seq, mp)

    def at_x(off):
        return (y, seq, lax.rem(x + off, 4) * 2 + zl)

    def at_z(off):
        zz = lax.rem(z + off, 8)
        return (y, (zz // 2) * 2 + c, x * 2 + zz % 2)

    sibling = (y, zh * 2 + 1 - c, mp)

    def copy(src, dst, send, recv, to):
        return pltpu.make_async_remote_copy(
            src_ref=src, dst_ref=dst, send_sem=ss.at[send], recv_sem=rs.at[recv],
            device_id=to, device_id_type=MESH,
        )

    pending = []

    def send(src, dst, sem, to):
        cp = copy(src, dst, sem, sem, to)
        cp.start()
        pending.append(cp)
        return cp

    def arrived(dst, sem):
        copy(dst, dst, sem, sem, sibling).wait_recv()

    rows_of = lambda s: pl.ds(pl.multiple_of(s * HD, HD), HD)
    own_rows = rows_of(seq)
    fetches = [
        pltpu.make_async_copy(src, dst, lsem.at[n])
        for n, (src, dst) in enumerate(
            (
                (prompt_hbm, prompt_of),
                (length_hbm, lengths),
                (q_hbm.at[0], q_ref),
                (kv_hbm.at[0], kv_ref),
                (k_hbm.at[0], kb.at[own_rows, 0:HD]),
                (v_hbm.at[0], kb.at[own_rows, HD : 2 * HD]),
            )
        )
    ]
    for cp in fetches:
        cp.start()
    keeps = zl == c
    w_local = pltpu.make_async_copy(w_ref, wb.at[y, zl], lsem.at[len(fetches)])

    @pl.when(keeps)
    def _():
        w_local.start()

    barrier = pltpu.get_barrier_semaphore()
    peers = [at_y(1), at_y(2), at_y(3), sibling, at_x(1), at_x(2), at_x(3)]
    peers += [at_z(m) for m in (4, 3, 5, 2, 6, 1, 7)]
    peers.append((y, zh * 2 + 1 - c, x * 2 + 1 - zl))
    for peer in peers:
        pl.semaphore_signal(barrier, inc=1, device_id=peer, device_id_type=MESH)

    for cp in fetches[4:]:
        cp.wait()
    pl.semaphore_wait(barrier, len(peers))

    swaps = []
    for j in range(2):
        rows = pl.ds(j * half_k, half_k)
        swaps.append(
            copy(
                w_ref.at[rows], wb.at[y, zl, rows], S_WSWAP(j), S_WSWAP(0),
                (y, zh * 2 + j, x * 2 + 1 - zl),
            )
        )

    def swap_start():
        @pl.when(jnp.logical_not(keeps))
        def _():
            for cp in swaps:
                cp.start()

    for m in (2, 1, 3):
        send(kb.at[own_rows], kb.at[own_rows], S_K(m), at_z(2 * m))
    send(kb.at[own_rows], kb.at[own_rows], S_KS(0), sibling)
    for cp in fetches[:4]:
        cp.wait()
    source = y * 8 + seq
    for k in range(4):
        prompt = lax.rem(y + k, 4)
        slot = jnp.int32(0)
        for j in range(1, 4):
            slot = jnp.where(prompt_of[j, source] == prompt, j, slot)
        to, at = (qb, y) if k == 0 else (qs, k)
        to[at, :, 0:width] = q_ref[slot]
        pair = kv_ref[slot]
        to[at, :, width : width + HD] = pair[:, 0, :]
        to[at, :, width + HD : width + 2 * HD] = pair[:, 1, :]

    for k in (2, 1, 3):
        send(qs.at[k], qb.at[y], S_Q(k), at_y(k))

    w_sib = copy(w_ref, wb.at[y, zl], S_WSIB(0), S_WSIB(0), sibling)

    @pl.when(keeps)
    def _():
        w_sib.start()
        w_local.wait()

    @pl.when(jnp.logical_not(keeps))
    def _():
        w_sib.wait_recv()

    mine = lambda core: pl.ds(pl.multiple_of(core * half_k, half_k), half_k)
    quarter = half_k // 2
    part = lambda core, h: pl.ds(pl.multiple_of(core * half_k + h * quarter, quarter), quarter)
    late = 1 - zl

    def w_start(r, kh):
        block = wb.at[y, kh, mine(c)]
        send(block, block, S_WRING(r, 0, 0), at_y(1))
        send(block, block, S_WRING(r, 0, 1), at_y(3))

    def w_share(r, n, slot):
        send(slot, slot, S_WSHARE(r, n), sibling)

    def w_relay(r, kh):
        left, right = lax.rem(y + 3, 4), lax.rem(y + 1, 4)
        arrived(wb.at[left, kh, mine(c)], S_WRING(r, 0, 0))
        slot = wb.at[left, kh, part(c, 0)]
        send(slot, slot, S_WRING(r, 1, 0), at_y(1))
        w_share(r, 1, wb.at[left, kh, mine(c)])
        arrived(wb.at[right, kh, mine(c)], S_WRING(r, 0, 1))
        slot = wb.at[right, kh, part(c, 1)]
        send(slot, slot, S_WRING(r, 1, 1), at_y(3))
        w_share(r, 2, wb.at[right, kh, mine(c)])

    def w_finish(r, kh):
        far = lax.rem(y + 2, 4)
        for h in range(2):
            slot = wb.at[far, kh, part(c, h)]
            arrived(slot, S_WRING(r, 1, h))
            w_share(r, 3 + h, slot)

    def w_shared(r, n):
        kh = zl if r == 0 else 1 - zl
        other = 1 - c
        if n == 0:
            slot = wb.at[y, kh, mine(other)]
        elif n == 1:
            slot = wb.at[lax.rem(y + 3, 4), kh, mine(other)]
        elif n == 2:
            slot = wb.at[lax.rem(y + 1, 4), kh, mine(other)]
        else:
            slot = wb.at[lax.rem(y + 2, 4), kh, part(other, n - 3)]
        arrived(slot, S_WSHARE(r, n))

    def w_near():
        w_shared(1, 0)
        for r in range(2):
            w_shared(r, 1)
            w_shared(r, 2)

    def w_far():
        for r in range(2):
            w_shared(r, 3)
            w_shared(r, 4)

    def k_forward():
        for m in (1, 3, 2):
            block = rows_of(lax.rem(zh + 4 - m, 4) * 2 + c)
            arrived(kb.at[block], S_K(m))
            send(kb.at[block], kb.at[block], S_KS(m), sibling)

    def k_shared():
        for m in range(4):
            arrived(kb.at[rows_of(lax.rem(zh + 4 - m, 4) * 2 + 1 - c)], S_KS(m))

    def swap_end():
        arrived(wb.at[y, late, mine(c)], S_WSWAP(0))
        w_start(1, late)
        w_share(1, 0, wb.at[y, late, mine(c)])

    factor = math.log2(math.e) / math.sqrt(HD)

    def attend(i):
        d = lax.rem(y + Y_OFF[i], 4)
        if i:
            arrived(qb.at[d], S_Q((4 - Y_OFF[i]) % 4))
        src = d * 8 + seq
        length = jnp.int32(0)
        for j in range(4):
            length = length + jnp.where(prompt_of[j, src] == y, lengths[j, src], 0)
        q = jnp.concatenate([qb[d, :, h * HD : (h + 1) * HD] for h in range(heads)], axis=0)
        near_k = qb[d, :, width : width + HD]
        near_v = qb[d, :, width + HD : width + 2 * HD]
        nt = (((1,), (1,)), ((), ()))
        far = lax.dot_general(q, kb[:, 0:HD], nt, preferred_element_type=jnp.float32)
        near = lax.dot_general(q, near_k, nt, preferred_element_type=jnp.float32)
        token = lax.rem(lax.broadcasted_iota(jnp.int32, near.shape, 0), cap)
        key = lax.broadcasted_iota(jnp.int32, near.shape, 1)
        near = jnp.where(token >= key, near, -jnp.inf)
        top = jnp.maximum(
            jnp.max(far, axis=1, keepdims=True), jnp.max(near, axis=1, keepdims=True)
        )
        far = jnp.exp2((far - top) * factor)
        near = jnp.exp2((near - top) * factor)
        total = jnp.sum(far, axis=1, keepdims=True) + jnp.sum(near, axis=1, keepdims=True)
        result = jnp.dot(far.astype(jnp.bfloat16), kb[:, HD : 2 * HD], preferred_element_type=jnp.float32)
        result = result + jnp.dot(
            near.astype(jnp.bfloat16), near_v, preferred_element_type=jnp.float32
        )
        row = lax.rem(lax.broadcasted_iota(jnp.int32, result.shape, 0), cap)
        result = jnp.where(row < length, result / total, 0.0).astype(jnp.bfloat16)
        for h in range(heads):
            ab[zh, zl, i * cap : (i + 1) * cap, h * HD : (h + 1) * HD] = (
                result[h * cap : (h + 1) * cap]
            )

    def a_slot(b, off, h=None):
        zz = lax.rem(z + off + 8, 8)
        first, size = BATCHES[b][0] * cap, len(BATCHES[b]) * cap
        if h is not None:
            size = size // 2
            first = first + h * size
        return ab.at[zz // 2, zz % 2, first : first + size]

    def a_start(b):
        for i in BATCHES[b]:
            attend(i)
        slot = a_slot(b, 0)
        send(slot, slot, S_A(b, 0, 0), at_z(1))
        send(slot, slot, S_A(b, 0, 1), at_z(7))

    def a_relay(b, s):
        slot = a_slot(b, -s)
        arrived(slot, S_A(b, s - 1, 0))
        if s == 3:
            slot = a_slot(b, -s, 0)
        send(slot, slot, S_A(b, s, 0), at_z(1))
        slot = a_slot(b, s)
        arrived(slot, S_A(b, s - 1, 1))
        if s == 3:
            slot = a_slot(b, s, 1)
        send(slot, slot, S_A(b, s, 1), at_z(7))

    def a_last(b):
        for h in range(2):
            arrived(a_slot(b, 4, h), S_A(b, 3, h))

    def pair(p):
        off = (0, 3 - 2 * zl, 1 + 2 * zl, 2)[p]
        return lax.rem(zh + off, 4)

    def span(p, g):
        return (LAST if p == 3 else GROUPS)[g]

    def cols(p, g):
        first, last = span(p, g)
        return slice(first * columns, last * columns)

    def chunk_of(xx):
        u = lax.rem(xx - y + 4, 4)
        return u + u // 2 - 2 * (u // 2) * (u % 2)

    def block_of(xx):
        return pl.ds(pl.multiple_of(chunk_of(xx) * cap, cap), cap)

    def project(p, g):
        zz = pair(p)
        for k in range(*span(p, g)):
            yk = lax.rem(y + Y_OFF[k], 4)
            value = jnp.dot(ab[zz, 0], wb[yk, 0], preferred_element_type=jnp.float32)
            value = value + jnp.dot(ab[zz, 1], wb[yk, 1], preferred_element_type=jnp.float32)
            cs[p, :, k * columns : (k + 1) * columns] = value.astype(jnp.bfloat16)
        for off in (2, 1, 3):
            rows = block_of(lax.rem(x + off, 4))
            send(
                cs.at[p, rows, cols(p, g)], rb.at[p, off, :, cols(p, g)], S_R(p, g, off), at_x(off)
            )

    def reduce(p, g):
        value = cs[p, block_of(x), cols(p, g)].astype(jnp.float32)
        for off in (1, 3, 2):
            arrived(rb.at[p, off, :, cols(p, g)], S_R(p, g, off))
            value = value + rb[p, off, :, cols(p, g)].astype(jnp.float32)
        fs[p, :, cols(p, g)] = value.astype(jnp.bfloat16)
        zz = pair(p)
        for t in range(2):
            half = slice(t * half_cap, (t + 1) * half_cap)
            if p == 0:
                @pl.when(zl == t)
                def _():
                    gb[z, :, cols(p, g)] = fs[p, half, cols(p, g)]
        if p == 0:
            half = pl.ds(pl.multiple_of(late * half_cap, half_cap), half_cap)
            off = 1 + 6 * zl
            send(
                fs.at[p, half, cols(p, g)], gb.at[z, :, cols(p, g)], S_G(g, 0) + off,
                (y, zz * 2 + c, x * 2 + late),
            )
        else:
            for t in range(2):
                half = slice(t * half_cap, (t + 1) * half_cap)
                off = lax.rem(zz * 2 + t - z + 8, 8)
                send(
                    fs.at[p, half, cols(p, g)], gb.at[z, :, cols(p, g)], S_G(g, 0) + off,
                    (y, zz * 2 + c, x * 2 + t),
                )

    def collect(p, g):
        zz = lax.rem(zh + (0, 1, 3, 2)[p], 4) * 2
        first, last = span(p, g)
        for t in range(2):
            src = zz + t
            if p:
                arrived(gb.at[src, :, cols(p, g)], S_G(g, 0) + lax.rem(z - src + 8, 8))
            elif t == 0:
                partner = z + 1 - 2 * zl
                off = 7 - 6 * zl
                arrived(gb.at[partner, :, cols(p, g)], S_G(g, 0) + off)
        for t in range(2):
            src = zz + t
            for k in range(first, last):
                yk = lax.rem(y + Y_OFF[k], 4)
                place = pl.ds(pl.multiple_of((yk * 8 + src) * columns, columns), columns)
                out_ref[:, place] = gb[src, :, k * columns : (k + 1) * columns]

    def drain(keep=0):
        while len(pending) > keep:
            pending.pop(0).wait_send()

    batches = range(len(BATCHES))
    w_start(0, zl)
    swap_start()
    k_forward()
    k_shared()
    a_start(0)
    swap_end()
    for b in batches[1:]:
        a_start(b)
    for b in batches:
        a_relay(b, 1)
    w_relay(0, zl)
    a_relay(0, 2)
    w_relay(1, late)
    for b in batches[1:]:
        a_relay(b, 2)
    w_near()
    project(0, 0)
    project(1, 0)
    for b in batches:
        a_relay(b, 3)
    project(2, 0)
    w_finish(0, zl)
    w_finish(1, late)
    w_far()
    project(0, 1)
    project(1, 1)
    project(2, 1)
    reduce(0, 0)
    reduce(1, 0)
    drain(18)
    for b in batches:
        a_last(b)
    for g in range(len(LAST)):
        project(3, g)
    reduce(0, 1)
    reduce(1, 1)
    reduce(2, 0)
    reduce(2, 1)
    for g in range(len(LAST)):
        reduce(3, g)
    for p in range(3):
        for g in range(len(GROUPS)):
            collect(p, g)
    drain(8)
    for g in range(len(LAST)):
        collect(3, g)

    drain()

    @pl.when(keeps)
    def _():
        w_sib.wait_send()

    @pl.when(jnp.logical_not(keeps))
    def _():
        for cp in swaps:
            cp.wait_send()


def local(queries, resp_kv, prompt_keys, prompt_values, out_weight, lengths, prompt_of):
    slots, cap, width = queries.shape[1:]
    tokens = prompt_keys.shape[1]
    k_rows, columns = out_weight.shape
    packed = width + 2 * HD
    bf = jnp.bfloat16
    hbm = pl.BlockSpec(memory_space=pltpu.HBM)
    return pl.pallas_call(
        kernel,
        out_shape=jax.ShapeDtypeStruct((16, 32 * columns), bf),
        in_specs=[hbm] * 7,
        out_specs=pl.BlockSpec(memory_space=pltpu.VMEM),
        scratch_shapes=[
            pltpu.SMEM(prompt_of.shape[::-1], jnp.int32),
            pltpu.SMEM(lengths.shape[::-1], jnp.int32),
            pltpu.VMEM((slots, cap, width), bf),
            pltpu.VMEM((slots, cap, 2, HD), bf),
            pltpu.VMEM((4, cap, packed), bf),
            pltpu.VMEM((4, cap, packed), bf),
            pltpu.VMEM((8 * tokens, 2 * HD), bf),
            pltpu.VMEM((4, 2, k_rows, columns), bf),
            pltpu.VMEM((4, 2, 4 * cap, width), bf),
            pltpu.VMEM((4, 4 * cap, 4 * columns), bf),
            pltpu.VMEM((4, 4, cap, 4 * columns), bf),
            pltpu.VMEM((4, cap, 4 * columns), bf),
            pltpu.VMEM((8, cap // 2, 4 * columns), bf),
            pltpu.SemaphoreType.DMA((N_SEM,)),
            pltpu.SemaphoreType.DMA((N_SEM,)),
            pltpu.SemaphoreType.DMA((8,)),
        ],
        compiler_params=pltpu.CompilerParams(
            collective_id=0, has_side_effects=True, vmem_limit_bytes=48 * 2**20
        ),
        cost_estimate=pl.CostEstimate(
            flops=2_700_000_000, bytes_accessed=2_000_000, transcendentals=1_100_000
        ),
        name="attend_project",
    )(*[
        pltpu.with_memory_space_constraint(a, pltpu.HBM)
        for a in (
            prompt_of.T, lengths.T, queries, resp_kv, prompt_keys, prompt_values, out_weight
        )
    ])


def solution(mesh):
    placed = (
        P(("dp", "seq"), None, None, "mp"),
        P(("dp", "seq"), None, None, None, "mp"),
        P("dp", "seq", "mp"),
        P("dp", "seq", "mp"),
        P("mp", ("dp", "seq")),
        P(),
        P(),
    )
    return jax.shard_map(
        local, mesh=mesh, in_specs=placed, out_specs=P(("dp", "seq", "mp"), None), check_vma=False
    )
```

```python
import math

import jax
import jax.numpy as jnp
from jax import lax
from jax.experimental import pallas as pl
from jax.experimental.pallas import tpu as pltpu
from jax.sharding import PartitionSpec as P

HD = 128
MESH = pl.DeviceIdType.MESH
Y_OFF = (0, 1, 3, 2)
BATCHES = ((0, 1), (2, 3))
GROUPS = ((0, 3), (3, 4))
LAST = ((0, 1), (1, 2), (2, 3), (3, 4))


class Ids:
    def __init__(self):
        self.n = 0

    def take(self, *dims):
        base = self.n
        size = math.prod(dims)
        self.n += size

        def at(*idx):
            flat = 0
            for d, i in zip(dims, idx):
                flat = flat * d + i
            return base + flat

        return at


IDS = Ids()
S_Q = IDS.take(4)
S_K = IDS.take(4)
S_KS = IDS.take(4)
S_WSIB = IDS.take(1)
S_WSWAP = IDS.take(2)
S_WRING = IDS.take(2, 2, 2)
S_WSHARE = IDS.take(2, 5)
S_A = IDS.take(len(BATCHES), 4, 2)
S_R = IDS.take(4, 4, 4)
S_G = IDS.take(4, 8)
N_SEM = IDS.n


def kernel(
    prompt_hbm, length_hbm, q_hbm, kv_hbm, k_hbm, v_hbm, w_ref, out_ref,
    prompt_of, lengths, q_ref, kv_ref,
    qs, qb, kb, wb, ab, cs, rb, fs, gb, ss, rs, lsem,
):
    y = lax.axis_index("dp")
    seq = lax.axis_index("seq")
    mp = lax.axis_index("mp")
    zh, c = seq // 2, seq % 2
    x, zl = mp // 2, mp % 2
    z = zh * 2 + zl
    half_k = w_ref.shape[0] // 2
    columns = w_ref.shape[1]
    cap = q_ref.shape[1]
    width = q_ref.shape[2]
    heads = width // HD
    half_cap = cap // 2

    def at_y(off):
        return (lax.rem(y + off, 4), seq, mp)

    def at_x(off):
        return (y, seq, lax.rem(x + off, 4) * 2 + zl)

    def at_z(off):
        zz = lax.rem(z + off, 8)
        return (y, (zz // 2) * 2 + c, x * 2 + zz % 2)

    sibling = (y, zh * 2 + 1 - c, mp)

    def copy(src, dst, send, recv, to):
        return pltpu.make_async_remote_copy(
            src_ref=src, dst_ref=dst, send_sem=ss.at[send], recv_sem=rs.at[recv],
            device_id=to, device_id_type=MESH,
        )

    pending = []

    def send(src, dst, sem, to):
        cp = copy(src, dst, sem, sem, to)
        cp.start()
        pending.append(cp)
        return cp

    def arrived(dst, sem):
        copy(dst, dst, sem, sem, sibling).wait_recv()

    rows_of = lambda s: pl.ds(pl.multiple_of(s * HD, HD), HD)
    own_rows = rows_of(seq)
    fetches = [
        pltpu.make_async_copy(src, dst, lsem.at[n])
        for n, (src, dst) in enumerate(
            (
                (prompt_hbm, prompt_of),
                (length_hbm, lengths),
                (q_hbm.at[0], q_ref),
                (kv_hbm.at[0], kv_ref),
                (k_hbm.at[0], kb.at[own_rows, 0:HD]),
                (v_hbm.at[0], kb.at[own_rows, HD : 2 * HD]),
            )
        )
    ]
    for cp in fetches:
        cp.start()
    keeps = zl == c
    w_local = pltpu.make_async_copy(w_ref, wb.at[y, zl], lsem.at[len(fetches)])

    @pl.when(keeps)
    def _():
        w_local.start()

    barrier = pltpu.get_barrier_semaphore()
    peers = [at_y(1), at_y(2), at_y(3), sibling, at_x(1), at_x(2), at_x(3)]
    peers += [at_z(m) for m in (4, 3, 5, 2, 6, 1, 7)]
    peers.append((y, zh * 2 + 1 - c, x * 2 + 1 - zl))
    for peer in peers:
        pl.semaphore_signal(barrier, inc=1, device_id=peer, device_id_type=MESH)

    for cp in fetches[4:]:
        cp.wait()
    for cp in fetches[:4]:
        cp.wait()
    source = y * 8 + seq
    for k in range(4):
        prompt = lax.rem(y + k, 4)
        slot = jnp.int32(0)
        for j in range(1, 4):
            slot = jnp.where(prompt_of[j, source] == prompt, j, slot)
        to, at = (qb, y) if k == 0 else (qs, k)
        to[at, :, 0:width] = q_ref[slot]
        pair = kv_ref[slot]
        to[at, :, width : width + HD] = pair[:, 0, :]
        to[at, :, width + HD : width + 2 * HD] = pair[:, 1, :]

    pl.semaphore_wait(barrier, len(peers))

    swaps = []
    for j in range(2):
        rows = pl.ds(j * half_k, half_k)
        swaps.append(
            copy(
                w_ref.at[rows], wb.at[y, zl, rows], S_WSWAP(j), S_WSWAP(0),
                (y, zh * 2 + j, x * 2 + 1 - zl),
            )
        )

    def swap_start():
        @pl.when(jnp.logical_not(keeps))
        def _():
            for cp in swaps:
                cp.start()

    for m in (2, 1, 3):
        send(kb.at[own_rows], kb.at[own_rows], S_K(m), at_z(2 * m))
    send(kb.at[own_rows], kb.at[own_rows], S_KS(0), sibling)
    for k in (2, 1, 3):
        send(qs.at[k], qb.at[y], S_Q(k), at_y(k))

    w_sib = copy(w_ref, wb.at[y, zl], S_WSIB(0), S_WSIB(0), sibling)

    @pl.when(keeps)
    def _():
        w_sib.start()
        w_local.wait()

    @pl.when(jnp.logical_not(keeps))
    def _():
        w_sib.wait_recv()

    mine = lambda core: pl.ds(pl.multiple_of(core * half_k, half_k), half_k)
    quarter = half_k // 2
    part = lambda core, h: pl.ds(pl.multiple_of(core * half_k + h * quarter, quarter), quarter)
    late = 1 - zl

    def w_start(r, kh):
        block = wb.at[y, kh, mine(c)]
        send(block, block, S_WRING(r, 0, 0), at_y(1))
        send(block, block, S_WRING(r, 0, 1), at_y(3))

    def w_share(r, n, slot):
        send(slot, slot, S_WSHARE(r, n), sibling)

    def w_relay(r, kh):
        left, right = lax.rem(y + 3, 4), lax.rem(y + 1, 4)
        arrived(wb.at[left, kh, mine(c)], S_WRING(r, 0, 0))
        slot = wb.at[left, kh, part(c, 0)]
        send(slot, slot, S_WRING(r, 1, 0), at_y(1))
        w_share(r, 1, wb.at[left, kh, mine(c)])
        arrived(wb.at[right, kh, mine(c)], S_WRING(r, 0, 1))
        slot = wb.at[right, kh, part(c, 1)]
        send(slot, slot, S_WRING(r, 1, 1), at_y(3))
        w_share(r, 2, wb.at[right, kh, mine(c)])

    def w_finish(r, kh):
        far = lax.rem(y + 2, 4)
        for h in range(2):
            slot = wb.at[far, kh, part(c, h)]
            arrived(slot, S_WRING(r, 1, h))
            w_share(r, 3 + h, slot)

    def w_shared(r, n):
        kh = zl if r == 0 else 1 - zl
        other = 1 - c
        if n == 0:
            slot = wb.at[y, kh, mine(other)]
        elif n == 1:
            slot = wb.at[lax.rem(y + 3, 4), kh, mine(other)]
        elif n == 2:
            slot = wb.at[lax.rem(y + 1, 4), kh, mine(other)]
        else:
            slot = wb.at[lax.rem(y + 2, 4), kh, part(other, n - 3)]
        arrived(slot, S_WSHARE(r, n))

    def w_near():
        w_shared(1, 0)
        for r in range(2):
            w_shared(r, 1)
            w_shared(r, 2)

    def w_far():
        for r in range(2):
            w_shared(r, 3)
            w_shared(r, 4)

    def k_forward():
        for m in (1, 3, 2):
            block = rows_of(lax.rem(zh + 4 - m, 4) * 2 + c)
            arrived(kb.at[block], S_K(m))
            send(kb.at[block], kb.at[block], S_KS(m), sibling)

    def k_shared():
        for m in range(4):
            arrived(kb.at[rows_of(lax.rem(zh + 4 - m, 4) * 2 + 1 - c)], S_KS(m))

    def swap_end():
        arrived(wb.at[y, late, mine(c)], S_WSWAP(0))
        w_start(1, late)
        w_share(1, 0, wb.at[y, late, mine(c)])

    factor = math.log2(math.e) / math.sqrt(HD)

    def attend(i):
        d = lax.rem(y + Y_OFF[i], 4)
        if i:
            arrived(qb.at[d], S_Q((4 - Y_OFF[i]) % 4))
        src = d * 8 + seq
        length = jnp.int32(0)
        for j in range(4):
            length = length + jnp.where(prompt_of[j, src] == y, lengths[j, src], 0)
        q = jnp.concatenate([qb[d, :, h * HD : (h + 1) * HD] for h in range(heads)], axis=0)
        near_k = qb[d, :, width : width + HD]
        near_v = qb[d, :, width + HD : width + 2 * HD]
        nt = (((1,), (1,)), ((), ()))
        far = lax.dot_general(q, kb[:, 0:HD], nt, preferred_element_type=jnp.float32)
        near = lax.dot_general(q, near_k, nt, preferred_element_type=jnp.float32)
        token = lax.rem(lax.broadcasted_iota(jnp.int32, near.shape, 0), cap)
        key = lax.broadcasted_iota(jnp.int32, near.shape, 1)
        near = jnp.where(token >= key, near, -jnp.inf)
        top = jnp.maximum(
            jnp.max(far, axis=1, keepdims=True), jnp.max(near, axis=1, keepdims=True)
        )
        far = jnp.exp2((far - top) * factor)
        near = jnp.exp2((near - top) * factor)
        total = jnp.sum(far, axis=1, keepdims=True) + jnp.sum(near, axis=1, keepdims=True)
        result = jnp.dot(far.astype(jnp.bfloat16), kb[:, HD : 2 * HD], preferred_element_type=jnp.float32)
        result = result + jnp.dot(
            near.astype(jnp.bfloat16), near_v, preferred_element_type=jnp.float32
        )
        row = lax.rem(lax.broadcasted_iota(jnp.int32, result.shape, 0), cap)
        result = jnp.where(row < length, result / total, 0.0).astype(jnp.bfloat16)
        for h in range(heads):
            ab[zh, zl, i * cap : (i + 1) * cap, h * HD : (h + 1) * HD] = (
                result[h * cap : (h + 1) * cap]
            )

    def a_slot(b, off, h=None):
        zz = lax.rem(z + off + 8, 8)
        first, size = BATCHES[b][0] * cap, len(BATCHES[b]) * cap
        if h is not None:
            size = size // 2
            first = first + h * size
        return ab.at[zz // 2, zz % 2, first : first + size]

    def a_start(b):
        for i in BATCHES[b]:
            attend(i)
        slot = a_slot(b, 0)
        send(slot, slot, S_A(b, 0, 0), at_z(1))
        send(slot, slot, S_A(b, 0, 1), at_z(7))

    def a_relay(b, s):
        slot = a_slot(b, -s)
        arrived(slot, S_A(b, s - 1, 0))
        if s == 3:
            slot = a_slot(b, -s, 0)
        send(slot, slot, S_A(b, s, 0), at_z(1))
        slot = a_slot(b, s)
        arrived(slot, S_A(b, s - 1, 1))
        if s == 3:
            slot = a_slot(b, s, 1)
        send(slot, slot, S_A(b, s, 1), at_z(7))

    def a_last(b):
        for h in range(2):
            arrived(a_slot(b, 4, h), S_A(b, 3, h))

    def pair(p):
        off = (0, 3 - 2 * zl, 1 + 2 * zl, 2)[p]
        return lax.rem(zh + off, 4)

    def span(p, g):
        return (LAST if p == 3 else GROUPS)[g]

    def cols(p, g):
        first, last = span(p, g)
        return slice(first * columns, last * columns)

    def chunk_of(xx):
        u = lax.rem(xx - y + 4, 4)
        return u + u // 2 - 2 * (u // 2) * (u % 2)

    def block_of(xx):
        return pl.ds(pl.multiple_of(chunk_of(xx) * cap, cap), cap)

    def project(p, g):
        zz = pair(p)
        for k in range(*span(p, g)):
            yk = lax.rem(y + Y_OFF[k], 4)
            value = jnp.dot(ab[zz, 0], wb[yk, 0], preferred_element_type=jnp.float32)
            value = value + jnp.dot(ab[zz, 1], wb[yk, 1], preferred_element_type=jnp.float32)
            cs[p, :, k * columns : (k + 1) * columns] = value.astype(jnp.bfloat16)
        for off in (2, 1, 3):
            rows = block_of(lax.rem(x + off, 4))
            send(
                cs.at[p, rows, cols(p, g)], rb.at[p, off, :, cols(p, g)], S_R(p, g, off), at_x(off)
            )

    def reduce(p, g):
        value = cs[p, block_of(x), cols(p, g)].astype(jnp.float32)
        for off in (1, 3, 2):
            arrived(rb.at[p, off, :, cols(p, g)], S_R(p, g, off))
            value = value + rb[p, off, :, cols(p, g)].astype(jnp.float32)
        fs[p, :, cols(p, g)] = value.astype(jnp.bfloat16)
        zz = pair(p)
        for t in range(2):
            half = slice(t * half_cap, (t + 1) * half_cap)
            if p == 0:
                @pl.when(zl == t)
                def _():
                    gb[z, :, cols(p, g)] = fs[p, half, cols(p, g)]
        if p == 0:
            half = pl.ds(pl.multiple_of(late * half_cap, half_cap), half_cap)
            off = 1 + 6 * zl
            send(
                fs.at[p, half, cols(p, g)], gb.at[z, :, cols(p, g)], S_G(g, 0) + off,
                (y, zz * 2 + c, x * 2 + late),
            )
        else:
            for t in range(2):
                half = slice(t * half_cap, (t + 1) * half_cap)
                off = lax.rem(zz * 2 + t - z + 8, 8)
                send(
                    fs.at[p, half, cols(p, g)], gb.at[z, :, cols(p, g)], S_G(g, 0) + off,
                    (y, zz * 2 + c, x * 2 + t),
                )

    def collect(p, g):
        zz = lax.rem(zh + (0, 1, 3, 2)[p], 4) * 2
        first, last = span(p, g)
        for t in range(2):
            src = zz + t
            if p:
                arrived(gb.at[src, :, cols(p, g)], S_G(g, 0) + lax.rem(z - src + 8, 8))
            elif t == 0:
                partner = z + 1 - 2 * zl
                off = 7 - 6 * zl
                arrived(gb.at[partner, :, cols(p, g)], S_G(g, 0) + off)
        for t in range(2):
            src = zz + t
            for k in range(first, last):
                yk = lax.rem(y + Y_OFF[k], 4)
                place = pl.ds(pl.multiple_of((yk * 8 + src) * columns, columns), columns)
                out_ref[:, place] = gb[src, :, k * columns : (k + 1) * columns]

    def drain(keep=0):
        while len(pending) > keep:
            pending.pop(0).wait_send()

    batches = range(len(BATCHES))
    w_start(0, zl)
    swap_start()
    k_forward()
    k_shared()
    a_start(0)
    swap_end()
    for b in batches[1:]:
        a_start(b)
    for b in batches:
        a_relay(b, 1)
    w_relay(0, zl)
    a_relay(0, 2)
    w_relay(1, late)
    for b in batches[1:]:
        a_relay(b, 2)
    w_near()
    project(0, 0)
    project(1, 0)
    for b in batches:
        a_relay(b, 3)
    project(2, 0)
    w_finish(0, zl)
    w_finish(1, late)
    w_far()
    project(0, 1)
    project(1, 1)
    project(2, 1)
    reduce(0, 0)
    reduce(1, 0)
    drain(18)
    for b in batches:
        a_last(b)
    for g in range(len(LAST)):
        project(3, g)
    reduce(0, 1)
    reduce(1, 1)
    reduce(2, 0)
    reduce(2, 1)
    for g in range(len(LAST)):
        reduce(3, g)
    for p in range(3):
        for g in range(len(GROUPS)):
            collect(p, g)
    drain(8)
    for g in range(len(LAST)):
        collect(3, g)

    drain()

    @pl.when(keeps)
    def _():
        w_sib.wait_send()

    @pl.when(jnp.logical_not(keeps))
    def _():
        for cp in swaps:
            cp.wait_send()


def local(queries, resp_kv, prompt_keys, prompt_values, out_weight, lengths, prompt_of):
    slots, cap, width = queries.shape[1:]
    tokens = prompt_keys.shape[1]
    k_rows, columns = out_weight.shape
    packed = width + 2 * HD
    bf = jnp.bfloat16
    hbm = pl.BlockSpec(memory_space=pltpu.HBM)
    return pl.pallas_call(
        kernel,
        out_shape=jax.ShapeDtypeStruct((16, 32 * columns), bf),
        in_specs=[hbm] * 7,
        out_specs=pl.BlockSpec(memory_space=pltpu.VMEM),
        scratch_shapes=[
            pltpu.SMEM(prompt_of.shape[::-1], jnp.int32),
            pltpu.SMEM(lengths.shape[::-1], jnp.int32),
            pltpu.VMEM((slots, cap, width), bf),
            pltpu.VMEM((slots, cap, 2, HD), bf),
            pltpu.VMEM((4, cap, packed), bf),
            pltpu.VMEM((4, cap, packed), bf),
            pltpu.VMEM((8 * tokens, 2 * HD), bf),
            pltpu.VMEM((4, 2, k_rows, columns), bf),
            pltpu.VMEM((4, 2, 4 * cap, width), bf),
            pltpu.VMEM((4, 4 * cap, 4 * columns), bf),
            pltpu.VMEM((4, 4, cap, 4 * columns), bf),
            pltpu.VMEM((4, cap, 4 * columns), bf),
            pltpu.VMEM((8, cap // 2, 4 * columns), bf),
            pltpu.SemaphoreType.DMA((N_SEM,)),
            pltpu.SemaphoreType.DMA((N_SEM,)),
            pltpu.SemaphoreType.DMA((8,)),
        ],
        compiler_params=pltpu.CompilerParams(
            collective_id=0, has_side_effects=True, vmem_limit_bytes=48 * 2**20
        ),
        cost_estimate=pl.CostEstimate(
            flops=2_700_000_000, bytes_accessed=2_000_000, transcendentals=1_100_000
        ),
        name="attend_project",
    )(*[
        pltpu.with_memory_space_constraint(a, pltpu.HBM)
        for a in (
            prompt_of.T, lengths.T, queries, resp_kv, prompt_keys, prompt_values, out_weight
        )
    ])


def solution(mesh):
    placed = (
        P(("dp", "seq"), None, None, "mp"),
        P(("dp", "seq"), None, None, None, "mp"),
        P("dp", "seq", "mp"),
        P("dp", "seq", "mp"),
        P("mp", ("dp", "seq")),
        P(),
        P(),
    )
    return jax.shard_map(
        local, mesh=mesh, in_specs=placed, out_specs=P(("dp", "seq", "mp"), None), check_vma=False
    )
```

```python
import math

import jax
import jax.numpy as jnp
from jax import lax
from jax.experimental import pallas as pl
from jax.experimental.pallas import tpu as pltpu
from jax.sharding import PartitionSpec as P

HD = 128
MESH = pl.DeviceIdType.MESH
Y_OFF = (0, 1, 3, 2)
BATCHES = ((0, 1), (2, 3))
GROUPS = ((0, 3), (3, 4))
LAST = ((0, 1), (1, 2), (2, 3), (3, 4))


class Ids:
    def __init__(self):
        self.n = 0

    def take(self, *dims):
        base = self.n
        size = math.prod(dims)
        self.n += size

        def at(*idx):
            flat = 0
            for d, i in zip(dims, idx):
                flat = flat * d + i
            return base + flat

        return at


IDS = Ids()
S_Q = IDS.take(4)
S_K = IDS.take(4)
S_KS = IDS.take(4)
S_WSIB = IDS.take(1)
S_WSWAP = IDS.take(2)
S_WRING = IDS.take(2, 2, 2)
S_WSHARE = IDS.take(2, 5)
S_A = IDS.take(len(BATCHES), 4, 2)
S_R = IDS.take(4, 4, 4)
S_G = IDS.take(4, 8)
N_SEM = IDS.n


def kernel(
    prompt_hbm, length_hbm, q_hbm, kv_hbm, k_hbm, v_hbm, w_ref, out_ref,
    prompt_of, lengths, q_ref, kv_ref,
    qs, qb, kb, wb, ab, cs, rb, fs, gb, ss, rs, lsem,
):
    y = lax.axis_index("dp")
    seq = lax.axis_index("seq")
    mp = lax.axis_index("mp")
    zh, c = seq // 2, seq % 2
    x, zl = mp // 2, mp % 2
    z = zh * 2 + zl
    half_k = w_ref.shape[0] // 2
    columns = w_ref.shape[1]
    cap = q_ref.shape[1]
    width = q_ref.shape[2]
    heads = width // HD
    half_cap = cap // 2

    def at_y(off):
        return (lax.rem(y + off, 4), seq, mp)

    def at_x(off):
        return (y, seq, lax.rem(x + off, 4) * 2 + zl)

    def at_z(off):
        zz = lax.rem(z + off, 8)
        return (y, (zz // 2) * 2 + c, x * 2 + zz % 2)

    sibling = (y, zh * 2 + 1 - c, mp)

    def copy(src, dst, send, recv, to):
        return pltpu.make_async_remote_copy(
            src_ref=src, dst_ref=dst, send_sem=ss.at[send], recv_sem=rs.at[recv],
            device_id=to, device_id_type=MESH,
        )

    pending = []

    def send(src, dst, sem, to):
        cp = copy(src, dst, sem, sem, to)
        cp.start()
        pending.append(cp)
        return cp

    def arrived(dst, sem):
        copy(dst, dst, sem, sem, sibling).wait_recv()

    rows_of = lambda s: pl.ds(pl.multiple_of(s * HD, HD), HD)
    own_rows = rows_of(seq)
    fetches = [
        pltpu.make_async_copy(src, dst, lsem.at[n])
        for n, (src, dst) in enumerate(
            (
                (prompt_hbm, prompt_of),
                (length_hbm, lengths),
                (q_hbm.at[0], q_ref),
                (kv_hbm.at[0], kv_ref),
                (k_hbm.at[0], kb.at[own_rows, 0:HD]),
                (v_hbm.at[0], kb.at[own_rows, HD : 2 * HD]),
            )
        )
    ]
    for cp in fetches:
        cp.start()
    keeps = zl == c
    w_local = pltpu.make_async_copy(w_ref, wb.at[y, zl], lsem.at[len(fetches)])

    @pl.when(keeps)
    def _():
        w_local.start()

    barrier = pltpu.get_barrier_semaphore()
    peers = [at_y(1), at_y(2), at_y(3), sibling, at_x(1), at_x(2), at_x(3)]
    peers += [at_z(m) for m in (4, 3, 5, 2, 6, 1, 7)]
    peers.append((y, zh * 2 + 1 - c, x * 2 + 1 - zl))
    for peer in peers:
        pl.semaphore_signal(barrier, inc=1, device_id=peer, device_id_type=MESH)

    for cp in fetches[4:]:
        cp.wait()
    for cp in fetches[:4]:
        cp.wait()
    source = y * 8 + seq
    for k in range(4):
        prompt = lax.rem(y + k, 4)
        slot = jnp.int32(0)
        for j in range(1, 4):
            slot = jnp.where(prompt_of[j, source] == prompt, j, slot)
        to, at = (qb, y) if k == 0 else (qs, k)
        to[at, :, 0:width] = q_ref[slot]
        pair = kv_ref[slot]
        to[at, :, width : width + HD] = pair[:, 0, :]
        to[at, :, width + HD : width + 2 * HD] = pair[:, 1, :]

    pl.semaphore_wait(barrier, len(peers))

    swaps = []
    for j in range(2):
        rows = pl.ds(j * half_k, half_k)
        swaps.append(
            copy(
                w_ref.at[rows], wb.at[y, zl, rows], S_WSWAP(j), S_WSWAP(0),
                (y, zh * 2 + j, x * 2 + 1 - zl),
            )
        )

    def swap_start():
        @pl.when(jnp.logical_not(keeps))
        def _():
            for cp in swaps:
                cp.start()

    for m in (2, 1, 3):
        send(kb.at[own_rows], kb.at[own_rows], S_K(m), at_z(2 * m))
    send(kb.at[own_rows], kb.at[own_rows], S_KS(0), sibling)
    for k in (2, 1, 3):
        send(qs.at[k], qb.at[y], S_Q(k), at_y(k))

    w_sib = copy(w_ref, wb.at[y, zl], S_WSIB(0), S_WSIB(0), sibling)

    @pl.when(keeps)
    def _():
        w_sib.start()
        w_local.wait()

    @pl.when(jnp.logical_not(keeps))
    def _():
        w_sib.wait_recv()

    mine = lambda core: pl.ds(pl.multiple_of(core * half_k, half_k), half_k)
    quarter = half_k // 2
    part = lambda core, h: pl.ds(pl.multiple_of(core * half_k + h * quarter, quarter), quarter)
    late = 1 - zl

    def w_start(r, kh):
        block = wb.at[y, kh, mine(c)]
        send(block, block, S_WRING(r, 0, 0), at_y(1))
        send(block, block, S_WRING(r, 0, 1), at_y(3))

    def w_share(r, n, slot):
        send(slot, slot, S_WSHARE(r, n), sibling)

    def w_relay(r, kh):
        left, right = lax.rem(y + 3, 4), lax.rem(y + 1, 4)
        arrived(wb.at[left, kh, mine(c)], S_WRING(r, 0, 0))
        slot = wb.at[left, kh, part(c, 0)]
        send(slot, slot, S_WRING(r, 1, 0), at_y(1))
        w_share(r, 1, wb.at[left, kh, mine(c)])
        arrived(wb.at[right, kh, mine(c)], S_WRING(r, 0, 1))
        slot = wb.at[right, kh, part(c, 1)]
        send(slot, slot, S_WRING(r, 1, 1), at_y(3))
        w_share(r, 2, wb.at[right, kh, mine(c)])

    def w_finish(r, kh):
        far = lax.rem(y + 2, 4)
        for h in range(2):
            slot = wb.at[far, kh, part(c, h)]
            arrived(slot, S_WRING(r, 1, h))
            w_share(r, 3 + h, slot)

    def w_shared(r, n):
        kh = zl if r == 0 else 1 - zl
        other = 1 - c
        if n == 0:
            slot = wb.at[y, kh, mine(other)]
        elif n == 1:
            slot = wb.at[lax.rem(y + 3, 4), kh, mine(other)]
        elif n == 2:
            slot = wb.at[lax.rem(y + 1, 4), kh, mine(other)]
        else:
            slot = wb.at[lax.rem(y + 2, 4), kh, part(other, n - 3)]
        arrived(slot, S_WSHARE(r, n))

    def w_near():
        w_shared(1, 0)
        for r in range(2):
            w_shared(r, 1)
            w_shared(r, 2)

    def w_far():
        for r in range(2):
            w_shared(r, 3)
            w_shared(r, 4)

    def k_forward():
        for m in (1, 3, 2):
            block = rows_of(lax.rem(zh + 4 - m, 4) * 2 + c)
            arrived(kb.at[block], S_K(m))
            send(kb.at[block], kb.at[block], S_KS(m), sibling)

    def k_shared():
        for m in range(4):
            arrived(kb.at[rows_of(lax.rem(zh + 4 - m, 4) * 2 + 1 - c)], S_KS(m))

    def swap_end():
        arrived(wb.at[y, late, mine(c)], S_WSWAP(0))
        w_start(1, late)
        w_share(1, 0, wb.at[y, late, mine(c)])

    factor = math.log2(math.e) / math.sqrt(HD)

    def attend(i):
        d = lax.rem(y + Y_OFF[i], 4)
        if i:
            arrived(qb.at[d], S_Q((4 - Y_OFF[i]) % 4))
        src = d * 8 + seq
        length = jnp.int32(0)
        for j in range(4):
            length = length + jnp.where(prompt_of[j, src] == y, lengths[j, src], 0)
        q = jnp.concatenate([qb[d, :, h * HD : (h + 1) * HD] for h in range(heads)], axis=0)
        near_k = qb[d, :, width : width + HD]
        near_v = qb[d, :, width + HD : width + 2 * HD]
        nt = (((1,), (1,)), ((), ()))
        far = lax.dot_general(q, kb[:, 0:HD], nt, preferred_element_type=jnp.float32)
        near = lax.dot_general(q, near_k, nt, preferred_element_type=jnp.float32)
        token = lax.rem(lax.broadcasted_iota(jnp.int32, near.shape, 0), cap)
        key = lax.broadcasted_iota(jnp.int32, near.shape, 1)
        near = jnp.where(token >= key, near, -jnp.inf)
        top = jnp.maximum(
            jnp.max(far, axis=1, keepdims=True), jnp.max(near, axis=1, keepdims=True)
        )
        far = jnp.exp2((far - top) * factor)
        near = jnp.exp2((near - top) * factor)
        total = jnp.sum(far, axis=1, keepdims=True) + jnp.sum(near, axis=1, keepdims=True)
        result = jnp.dot(far.astype(jnp.bfloat16), kb[:, HD : 2 * HD], preferred_element_type=jnp.float32)
        result = result + jnp.dot(
            near.astype(jnp.bfloat16), near_v, preferred_element_type=jnp.float32
        )
        row = lax.rem(lax.broadcasted_iota(jnp.int32, result.shape, 0), cap)
        result = jnp.where(row < length, result / total, 0.0).astype(jnp.bfloat16)
        for h in range(heads):
            ab[zh, zl, i * cap : (i + 1) * cap, h * HD : (h + 1) * HD] = (
                result[h * cap : (h + 1) * cap]
            )

    def a_slot(b, off, h=None):
        zz = lax.rem(z + off + 8, 8)
        first, size = BATCHES[b][0] * cap, len(BATCHES[b]) * cap
        if h is not None:
            size = size // 2
            first = first + h * size
        return ab.at[zz // 2, zz % 2, first : first + size]

    def a_start(b):
        for i in BATCHES[b]:
            attend(i)
        slot = a_slot(b, 0)
        send(slot, slot, S_A(b, 0, 0), at_z(1))
        send(slot, slot, S_A(b, 0, 1), at_z(7))

    def a_relay(b, s):
        slot = a_slot(b, -s)
        arrived(slot, S_A(b, s - 1, 0))
        if s == 3:
            slot = a_slot(b, -s, 0)
        send(slot, slot, S_A(b, s, 0), at_z(1))
        slot = a_slot(b, s)
        arrived(slot, S_A(b, s - 1, 1))
        if s == 3:
            slot = a_slot(b, s, 1)
        send(slot, slot, S_A(b, s, 1), at_z(7))

    def a_last(b):
        for h in range(2):
            arrived(a_slot(b, 4, h), S_A(b, 3, h))

    def pair(p):
        off = (0, 3 - 2 * zl, 1 + 2 * zl, 2)[p]
        return lax.rem(zh + off, 4)

    def span(p, g):
        return (LAST if p == 3 else GROUPS)[g]

    def cols(p, g):
        first, last = span(p, g)
        return slice(first * columns, last * columns)

    def chunk_of(xx):
        u = lax.rem(xx - y + 4, 4)
        return u + u // 2 - 2 * (u // 2) * (u % 2)

    def block_of(xx):
        return pl.ds(pl.multiple_of(chunk_of(xx) * cap, cap), cap)

    def project(p, g):
        zz = pair(p)
        for k in range(*span(p, g)):
            yk = lax.rem(y + Y_OFF[k], 4)
            value = jnp.dot(ab[zz, 0], wb[yk, 0], preferred_element_type=jnp.float32)
            value = value + jnp.dot(ab[zz, 1], wb[yk, 1], preferred_element_type=jnp.float32)
            cs[p, :, k * columns : (k + 1) * columns] = value.astype(jnp.bfloat16)
        for off in (2, 1, 3):
            rows = block_of(lax.rem(x + off, 4))
            send(
                cs.at[p, rows, cols(p, g)], rb.at[p, off, :, cols(p, g)], S_R(p, g, off), at_x(off)
            )

    def reduce(p, g):
        value = cs[p, block_of(x), cols(p, g)].astype(jnp.float32)
        for off in (1, 3, 2):
            arrived(rb.at[p, off, :, cols(p, g)], S_R(p, g, off))
            value = value + rb[p, off, :, cols(p, g)].astype(jnp.float32)
        fs[p, :, cols(p, g)] = value.astype(jnp.bfloat16)
        zz = pair(p)
        for t in range(2):
            half = slice(t * half_cap, (t + 1) * half_cap)
            if p == 0:
                @pl.when(zl == t)
                def _():
                    gb[z, :, cols(p, g)] = fs[p, half, cols(p, g)]
        if p == 0:
            half = pl.ds(pl.multiple_of(late * half_cap, half_cap), half_cap)
            off = 1 + 6 * zl
            send(
                fs.at[p, half, cols(p, g)], gb.at[z, :, cols(p, g)], S_G(g, 0) + off,
                (y, zz * 2 + c, x * 2 + late),
            )
        else:
            for t in range(2):
                half = slice(t * half_cap, (t + 1) * half_cap)
                off = lax.rem(zz * 2 + t - z + 8, 8)
                send(
                    fs.at[p, half, cols(p, g)], gb.at[z, :, cols(p, g)], S_G(g, 0) + off,
                    (y, zz * 2 + c, x * 2 + t),
                )

    def collect(p, g):
        zz = lax.rem(zh + (0, 1, 3, 2)[p], 4) * 2
        first, last = span(p, g)
        for t in range(2):
            src = zz + t
            if p:
                arrived(gb.at[src, :, cols(p, g)], S_G(g, 0) + lax.rem(z - src + 8, 8))
            elif t == 0:
                partner = z + 1 - 2 * zl
                off = 7 - 6 * zl
                arrived(gb.at[partner, :, cols(p, g)], S_G(g, 0) + off)
        for t in range(2):
            src = zz + t
            for k in range(first, last):
                yk = lax.rem(y + Y_OFF[k], 4)
                place = pl.ds(pl.multiple_of((yk * 8 + src) * columns, columns), columns)
                out_ref[:, place] = gb[src, :, k * columns : (k + 1) * columns]

    def drain(keep=0):
        while len(pending) > keep:
            pending.pop(0).wait_send()

    batches = range(len(BATCHES))
    w_start(0, zl)
    swap_start()
    k_forward()
    k_shared()
    a_start(0)
    swap_end()
    for b in batches[1:]:
        a_start(b)
    a_relay(0, 1)
    w_relay(0, zl)
    a_relay(1, 1)
    a_relay(0, 2)
    w_relay(1, late)
    for b in batches[1:]:
        a_relay(b, 2)
    w_near()
    project(0, 0)
    project(1, 0)
    for b in batches:
        a_relay(b, 3)
    project(2, 0)
    w_finish(0, zl)
    w_finish(1, late)
    w_far()
    project(0, 1)
    project(1, 1)
    project(2, 1)
    reduce(0, 0)
    reduce(1, 0)
    drain(18)
    for b in batches:
        a_last(b)
    for g in range(len(LAST)):
        project(3, g)
    reduce(0, 1)
    reduce(1, 1)
    reduce(2, 0)
    reduce(2, 1)
    for g in range(len(LAST)):
        reduce(3, g)
    for p in range(3):
        for g in range(len(GROUPS)):
            collect(p, g)
    drain(8)
    for g in range(len(LAST)):
        collect(3, g)

    drain()

    @pl.when(keeps)
    def _():
        w_sib.wait_send()

    @pl.when(jnp.logical_not(keeps))
    def _():
        for cp in swaps:
            cp.wait_send()


def local(queries, resp_kv, prompt_keys, prompt_values, out_weight, lengths, prompt_of):
    slots, cap, width = queries.shape[1:]
    tokens = prompt_keys.shape[1]
    k_rows, columns = out_weight.shape
    packed = width + 2 * HD
    bf = jnp.bfloat16
    hbm = pl.BlockSpec(memory_space=pltpu.HBM)
    return pl.pallas_call(
        kernel,
        out_shape=jax.ShapeDtypeStruct((16, 32 * columns), bf),
        in_specs=[hbm] * 7,
        out_specs=pl.BlockSpec(memory_space=pltpu.VMEM),
        scratch_shapes=[
            pltpu.SMEM(prompt_of.shape[::-1], jnp.int32),
            pltpu.SMEM(lengths.shape[::-1], jnp.int32),
            pltpu.VMEM((slots, cap, width), bf),
            pltpu.VMEM((slots, cap, 2, HD), bf),
            pltpu.VMEM((4, cap, packed), bf),
            pltpu.VMEM((4, cap, packed), bf),
            pltpu.VMEM((8 * tokens, 2 * HD), bf),
            pltpu.VMEM((4, 2, k_rows, columns), bf),
            pltpu.VMEM((4, 2, 4 * cap, width), bf),
            pltpu.VMEM((4, 4 * cap, 4 * columns), bf),
            pltpu.VMEM((4, 4, cap, 4 * columns), bf),
            pltpu.VMEM((4, cap, 4 * columns), bf),
            pltpu.VMEM((8, cap // 2, 4 * columns), bf),
            pltpu.SemaphoreType.DMA((N_SEM,)),
            pltpu.SemaphoreType.DMA((N_SEM,)),
            pltpu.SemaphoreType.DMA((8,)),
        ],
        compiler_params=pltpu.CompilerParams(
            collective_id=0, has_side_effects=True, vmem_limit_bytes=48 * 2**20
        ),
        cost_estimate=pl.CostEstimate(
            flops=2_700_000_000, bytes_accessed=2_000_000, transcendentals=1_100_000
        ),
        name="attend_project",
    )(*[
        pltpu.with_memory_space_constraint(a, pltpu.HBM)
        for a in (
            prompt_of.T, lengths.T, queries, resp_kv, prompt_keys, prompt_values, out_weight
        )
    ])


def solution(mesh):
    placed = (
        P(("dp", "seq"), None, None, "mp"),
        P(("dp", "seq"), None, None, None, "mp"),
        P("dp", "seq", "mp"),
        P("dp", "seq", "mp"),
        P("mp", ("dp", "seq")),
        P(),
        P(),
    )
    return jax.shard_map(
        local, mesh=mesh, in_specs=placed, out_specs=P(("dp", "seq", "mp"), None), check_vma=False
    )
```
